256 devices in a mesh: seq: 64 (over z, x, core), ch: 4 (over y).
Axes of the slice: x: 4, y: 4, z: 8, core: 2. Of those that a mesh axis runs over, the one named last changes fastest.
Arguments:
- tokens: bfloat16 [16384, 4096], P('seq', 'ch'), may hold values from -6 to 6
- w_value: bfloat16 [4096, 2048], P(None, 'ch'), may hold values from -0.09375 to 0.09375
- w_gate: bfloat16 [4096, 2048], P(None, 'ch'), may hold values from -0.09375 to 0.09375
- short_value: float32 [3, 2048], P(None, 'ch'), may hold values from -3.5 to 3.5
- short_gate: float32 [3, 2048], P(None, 'ch'), may hold values from -3.5 to 3.5
- skip_bias: float32 [2048], P('ch'), may hold values from 0.5 to 1.5
- long_filter: float32 [16384, 2048], P('seq', 'ch'), may hold values from -0.046875 to 0.046875
- grad_out: bfloat16 [16384, 2048], P('seq', 'ch'), may hold values from -0.046875 to 0.046875
Outputs:
- output: bfloat16 [16384, 2048], P('seq', 'ch')
- filter_grad: float32 [16384, 2048], P('seq', 'ch')
The draws below stay inside these ranges and needn't reach their ends.
All inputs are finite; a program needn't handle non-finite values.
Results may differ from the reference program's by a relative error of at most 0.0095.
Values may be sent and summed in bfloat16 or wider, within the bound.
A program may use at most 128 MiB of HBM per device.

```python
import jax
import jax.numpy as jnp
from jax import lax

D = 4096
C = 2048
TOKENS = 16384


def block_scale(rng, extent, cuts, smallest, top_value):
    def one(dim, blocks):
        steps = jax.random.uniform(jax.random.fold_in(jax.random.fold_in(rng, 6), dim), (blocks,), jnp.float32, smallest / len(cuts), top_value / len(cuts))
        return jnp.repeat(jnp.exp(steps), extent[dim] // blocks).reshape((-1,) + (1,) * (len(extent) - dim - 1))

    loudness = one(*cuts[0])
    for cut in cuts[1:]:
        loudness = loudness * one(*cut)
    return loudness


def scatter_about(own_key, shape, width, bound, split=(), held_as=jnp.bfloat16):
    values = jax.random.normal(own_key, shape, jnp.float32) * width
    if len(split) > 0:
        values = block_scale(own_key, shape, split, -0.22, 0.18) * values
    return jnp.clip(values, min=-bound, max=bound).astype(held_as)


def setup_inputs(seed: int = 0) -> dict:
    key_of = jax.random.split(jax.random.key(seed), 9)
    tokens = scatter_about(key_of[0], (TOKENS, D), 1.0, 6.0, ((0, 64), (1, 4)))
    w_value = scatter_about(key_of[1], (D, C), D ** -0.5, 0.09375, ((1, 4),))
    w_gate = scatter_about(key_of[2], (D, C), D ** -0.5, 0.09375, ((1, 4),))
    short_value = scatter_about(key_of[3], (3, C), 3 ** -0.5, 3.5, ((1, 4),), jnp.float32)
    short_gate = scatter_about(key_of[4], (3, C), 3 ** -0.5, 3.5, ((1, 4),), jnp.float32)
    skip_bias = jnp.clip(0.5 + 1.0 * jax.random.uniform(key_of[5], (C,), jnp.float32) ** block_scale(key_of[5], (C,), ((0, 4),), -0.2, 0.2), 0.5, 1.5)
    long_filter = scatter_about(key_of[6], (TOKENS, C), TOKENS ** -0.5, 0.046875, ((0, 64), (1, 4)), jnp.float32)
    grad_out = scatter_about(key_of[7], (TOKENS, C), TOKENS ** -0.5, 0.046875, ((0, 64), (1, 4)))
    return dict(tokens=tokens, w_value=w_value, w_gate=w_gate, short_value=short_value, short_gate=short_gate, skip_bias=skip_bias, long_filter=long_filter, grad_out=grad_out)


def short_filter(projected, kernel):
    widened = projected.astype(jnp.float32)
    padded = jnp.pad(widened, ((2, 0), (0, 0)))
    return kernel[0] * widened + kernel[1] * padded[1:-1] + kernel[2] * padded[:-2]


def reference(tokens, w_value, w_gate, short_value, short_gate, skip_bias, long_filter, grad_out):
    seq_length = tokens.shape[0]
    fft_length = 2 * seq_length
    proj_value = lax.optimization_barrier(jnp.dot(tokens, w_value, preferred_element_type=jnp.float32).astype(jnp.bfloat16))
    proj_gate = lax.optimization_barrier(jnp.dot(tokens, w_gate, preferred_element_type=jnp.float32).astype(jnp.bfloat16))
    value_act = short_filter(proj_value, short_value)
    gate_act = short_filter(proj_gate, short_gate)
    value_spec = jnp.fft.rfft(value_act, n=fft_length, axis=0)
    filter_spec = jnp.fft.rfft(long_filter, n=fft_length, axis=0)
    long_conv = jnp.fft.irfft(value_spec * filter_spec, n=fft_length, axis=0)[:seq_length]
    mixed_sum = long_conv + skip_bias * value_act
    output = (gate_act * mixed_sum).astype(jnp.bfloat16)
    grad_mixed = grad_out.astype(jnp.float32) * gate_act
    grad_spec = jnp.fft.rfft(grad_mixed, n=fft_length, axis=0)
    filter_grad = jnp.fft.irfft(grad_spec * jnp.conj(value_spec), n=fft_length, axis=0)[:seq_length]
    return output, filter_grad
```

```python
import functools
import math

import jax
import jax.numpy as jnp
import numpy as np
from jax import lax
from jax.experimental import pallas as pl
from jax.experimental.pallas import tpu as pltpu
from jax.sharding import PartitionSpec as P

MESH = pl.DeviceIdType.MESH
F32 = jnp.float32
BF16 = jnp.bfloat16
HALO = 16


def tables(blocks, half):
    count = 2 * blocks
    row = np.arange(count)
    q = 2 * (row % blocks) + row // blocks
    k = np.arange(count)
    angle = 2 * np.pi * ((k[:, None] * q[None, :]) % count + q[None, :] / 4) / count
    first = np.concatenate([np.cos(angle), -np.sin(angle)], axis=0)
    last = np.concatenate([np.cos(angle).T, -np.sin(angle).T], axis=1) / (count * half)
    l = np.arange(half)
    twist = 2 * np.pi * (k[:, None] + 0.25) * l[None, :] / (count * half)
    turn = 2 * np.pi * ((l[:, None] * l[None, :]) % half) / half
    c, s = np.cos(turn), np.sin(turn)
    second = np.block([[c, -s], [s, c]])
    third = np.block([[c, s], [-s, c]])
    return (
        jnp.asarray(first, BF16),
        jnp.asarray(second, BF16),
        jnp.asarray(third, BF16),
        jnp.asarray(last, BF16),
        jnp.asarray(np.stack([np.cos(twist), np.sin(twist)]), F32),
    )


def dot(a, b):
    return jnp.dot(a, b, preferred_element_type=F32)


def kernel(
    n, yn,
    tok_ref, wv_ref, wg_ref, taps_ref, skip_ref, filt_ref, gout_ref,
    first_ref, second_ref, third_ref, last_ref, twist_ref,
    out_ref, fgrad_ref,
    tok, wall, taps, skip, filt, gout, first, second, third, last, twist,
    acc, proj, tail, tail_in, value, gate,
    fsend, frecv, vsend, vrecv, csend, crecv, gsend, grecv,
    wide, vwide, mid, spec_v, spec_h, spec_g,
    loc_sem, w_sem, ag_send, ag_recv, tail_sem, f_sem, v_send, v_recv, c_sem, g_sem,
):
    seq = lax.axis_index("seq")
    ch = lax.axis_index("ch")
    rows, dl = tok_ref.shape
    cl = wv_ref.shape[1]
    half = rows // 2
    cpd = cl // n
    count = 2 * n
    right, left = lax.rem(ch + 1, yn), lax.rem(ch + yn - 1, yn)
    far = lax.rem(ch + 2, yn)
    right_id, left_id = (seq, right), (seq, left)

    def local(i, src, dst):
        return pltpu.make_async_copy(src, dst, loc_sem.at[i])

    locals_ = [
        local(0, filt_ref, filt),
        local(1, tok_ref, tok.at[ch]),
        local(2, first_ref, first),
        local(3, second_ref, second),
        local(4, third_ref, third),
        local(5, last_ref, last),
        local(6, twist_ref, twist),
        local(7, taps_ref, taps),
        local(8, skip_ref, skip),
        local(9, gout_ref, gout),
    ]
    for c in locals_[:2]:
        c.start()

    def weight_copies(i, src):
        at = pl.ds(pl.multiple_of(src * dl, dl), dl)
        return [
            pltpu.make_async_copy(wv_ref.at[at], wall.at[at, pl.ds(0, cl)], w_sem.at[2 * i]),
            pltpu.make_async_copy(wg_ref.at[at], wall.at[at, pl.ds(cl, cl)], w_sem.at[2 * i + 1]),
        ]

    weights = [weight_copies(i, s) for i, s in enumerate((ch, left, right, far))]
    for c in weights[0]:
        c.start()
    for c in locals_[2:]:
        c.start()
    for w in weights[1:]:
        for c in w:
            c.start()

    barrier = pltpu.get_barrier_semaphore()

    def greet(k, _):
        pl.semaphore_signal(barrier, inc=1, device_id=(lax.rem(seq + k, n), ch), device_id_type=MESH)
        return 0

    for device in (right_id, left_id):
        pl.semaphore_signal(barrier, inc=1, device_id=device, device_id_type=MESH)
    lax.fori_loop(1, n, greet, 0)

    locals_[0].wait()
    for h in range(2):
        turned = filt[pl.ds(h * half, half), :].T.reshape(n, cpd, half)
        wide[:, pl.ds(h * cpd, cpd), :] = turned
    fsend[...] = wide[...].astype(BF16)

    pl.semaphore_wait(barrier, n - 1 + 2)

    cut = half - HALO
    spans = (pl.ds(cut, rows - cut), pl.ds(0, cut))

    def ag(i, src, dst, device):
        return pltpu.make_async_remote_copy(
            src_ref=src, dst_ref=dst, send_sem=ag_send.at[i], recv_sem=ag_recv.at[i],
            device_id=device, device_id_type=MESH,
        )

    own = [
        [ag(4 * p, tok_ref.at[spans[p]], tok.at[ch, spans[p]], right_id),
         ag(4 * p + 1, tok_ref.at[spans[p]], tok.at[ch, spans[p]], left_id)]
        for p in range(2)
    ]
    low, high = pl.ds(0, dl // 2), pl.ds(dl // 2, dl // 2)

    def forwards(p):
        a, b = tok.at[left, spans[p], low], tok.at[right, spans[p], high]
        return [ag(4 * p + 2, a, a, right_id), ag(4 * p + 3, b, b, left_id)]

    onward = [forwards(p) for p in range(2)]

    def from_neighbour(p, side):
        src = (left, right)[side]
        return ag(4 * p + side, tok.at[src, spans[p]], tok.at[src, spans[p]], (right_id, left_id)[side])

    def from_far(p, side):
        part = tok.at[far, spans[p], (low, high)[side]]
        return ag(4 * p + 2 + side, part, part, (right_id, left_id)[side])

    for c in own[0]:
        c.start()

    def scatter(src, dst, send_sem, recv_sem):
        def one(k, _):
            to = lax.rem(seq + k, n)
            pltpu.make_async_remote_copy(
                src_ref=src.at[to], dst_ref=dst.at[seq], send_sem=send_sem, recv_sem=recv_sem,
                device_id=(to, ch), device_id_type=MESH,
            ).start()
            return 0

        lax.fori_loop(1, n, one, 0)
        dst[seq] = src[seq]

    def await_all(ref, sem):
        part = ref.at[pl.ds(0, n - 1)]
        pltpu.make_async_copy(part, part, sem).wait()

    scatter(fsend, frecv, f_sem.at[0], f_sem.at[1])

    def multiply(p, i, src):
        part = dot(tok[src, spans[p], :], wall[pl.ds(pl.multiple_of(src * dl, dl), dl), :])
        if i == 0:
            acc[spans[p], :] = part
        else:
            acc[spans[p], :] += part

    locals_[1].wait()
    for c in weights[0]:
        c.wait()
    multiply(0, 0, ch)
    multiply(1, 0, ch)

    for side in range(2):
        from_neighbour(0, side).wait_recv()
        onward[0][side].start()
    for c in own[1]:
        c.start()
    for w in weights[1:3]:
        for c in w:
            c.wait()
    multiply(0, 1, left)
    multiply(0, 2, right)

    for c in locals_[2:]:
        c.wait()

    tc, ts = twist[0], twist[1]

    def spectrum(load, spec):
        for pair in range(cpd // 2):
            c0, c1 = 2 * pair, 2 * pair + 1
            x = jnp.concatenate([load(c0), load(c1)], axis=1).astype(BF16)
            a = dot(first[...], x)
            for j, c in enumerate((c0, c1)):
                ar = a[:count, j * half:(j + 1) * half]
                ai = a[count:, j * half:(j + 1) * half]
                mid[pl.ds(c * count, count), pl.ds(0, half)] = (ar * tc + ai * ts).astype(BF16)
                mid[pl.ds(c * count, count), pl.ds(half, half)] = (ai * tc - ar * ts).astype(BF16)
        spec[...] = dot(mid[...], second[...])

    def restore(pr, pi, send):
        mid[:, pl.ds(0, half)] = pr.astype(BF16)
        mid[:, pl.ds(half, half)] = pi.astype(BF16)
        spec_g[...] = dot(mid[...], third[...])
        for pair in range(cpd // 2):
            both = []
            for c in (2 * pair, 2 * pair + 1):
                zr = spec_g[pl.ds(c * count, count), pl.ds(0, half)]
                zi = spec_g[pl.ds(c * count, count), pl.ds(half, half)]
                both.append(jnp.concatenate([zr * tc - zi * ts, zi * tc + zr * ts], axis=0).astype(BF16))
            y = dot(last[...], jnp.concatenate(both, axis=1))
            for j in range(2):
                for h in range(2):
                    vwide[pl.ds(h * cpd + 2 * pair + j, n, stride=2 * cpd), :] = (
                        y[h * n:(h + 1) * n, j * half:(j + 1) * half])
        send[...] = vwide[pl.ds(0, n * 2 * cpd), :].astype(BF16).reshape(n, 2 * cpd, half)

    await_all(frecv, f_sem.at[1])
    vwide[pl.ds(0, n * 2 * cpd), :] = frecv[...].astype(F32).reshape(n * 2 * cpd, half)
    spectrum(
        lambda c: jnp.concatenate(
            [vwide[pl.ds(h * cpd + c, n, stride=2 * cpd), :] for h in range(2)], axis=0),
        spec_h,
    )

    def project(p, h):
        for side in range(2):
            from_far(p, side).wait_recv()
        if p == 0:
            for c in weights[3]:
                c.wait()
        multiply(p, 3, far)
        rounded = acc[spans[p], :].astype(BF16)
        at = spans[p].start + HALO
        proj[pl.ds(at, spans[p].size), :] = rounded.astype(F32)

    def gather_short(h):
        def short(col, tap):
            cols = pl.ds(col, cl)
            return (
                taps[tap:tap + 1, :] * proj[pl.ds(HALO + h * half, half), cols]
                + taps[tap + 1:tap + 2, :] * proj[pl.ds(HALO - 1 + h * half, half), cols]
                + taps[tap + 2:tap + 3, :] * proj[pl.ds(HALO - 2 + h * half, half), cols]
            )

        at = pl.ds(h * half, half)
        v = short(0, 0)
        value[at, :] = v
        g = short(cl, 3)
        gate[at, :] = g
        mixed = gout[at, :].astype(F32) * g
        vsend[h] = jnp.concatenate(
            [v.T.reshape(n, cpd, half), mixed.T.reshape(n, cpd, half)], axis=1
        ).astype(BF16)
        scatter(vsend.at[h], vrecv.at[h], v_send.at[h], v_recv.at[h])

    project(0, 1)
    tail[...] = proj[pl.ds(rows, HALO), :].astype(BF16)
    tail_copy = pltpu.make_async_remote_copy(
        src_ref=tail, dst_ref=tail_in, send_sem=tail_sem.at[0], recv_sem=tail_sem.at[1],
        device_id=(lax.rem(seq + 1, n), ch), device_id_type=MESH,
    )
    tail_copy.start()
    gather_short(1)

    for side in range(2):
        from_neighbour(1, side).wait_recv()
        onward[1][side].start()
    multiply(1, 1, left)
    multiply(1, 2, right)
    tail_copy.wait_recv()
    proj[pl.ds(0, HALO), :] = jnp.where(seq > 0, tail_in[...].astype(F32), 0.0)
    project(1, 0)
    gather_short(0)

    for h in (1, 0):
        await_all(vrecv.at[h], v_recv.at[h])
    vwide[...] = vrecv[...].astype(F32).reshape(2 * n * 2 * cpd, half)

    def branch(offset):
        return lambda c: jnp.concatenate(
            [vwide[pl.ds(h * n * 2 * cpd + offset + c, n, stride=2 * cpd), :] for h in range(2)], axis=0)

    spectrum(branch(0), spec_v)
    spectrum(branch(cpd), spec_g)
    re, im = pl.ds(0, half), pl.ds(half, half)
    gr, gi = spec_g[:, re], spec_g[:, im]
    vr, vi = spec_v[:, re], spec_v[:, im]
    wide_g_r = gr * vr + gi * vi
    wide_g_i = gi * vr - gr * vi
    hr, hi = spec_h[:, re], spec_h[:, im]
    conv_r = vr * hr - vi * hi
    conv_i = vr * hi + vi * hr
    spec_v[:, re] = wide_g_r
    spec_v[:, im] = wide_g_i
    restore(conv_r, conv_i, csend)
    scatter(csend, crecv, c_sem.at[0], c_sem.at[1])
    restore(spec_v[:, re], spec_v[:, im], gsend)
    scatter(gsend, grecv, g_sem.at[0], g_sem.at[1])

    await_all(crecv, c_sem.at[1])
    wide[...] = crecv[...].astype(F32)
    for h in range(2):
        at = pl.ds(h * half, half)
        y = wide[:, pl.ds(h * cpd, cpd), :].reshape(cl, half).T
        out_ref[at, :] = (gate[at, :] * (y + skip[...] * value[at, :])).astype(BF16)
    await_all(grecv, g_sem.at[1])
    wide[...] = grecv[...].astype(F32)
    for h in range(2):
        at = pl.ds(h * half, half)
        fgrad_ref[at, :] = wide[:, pl.ds(h * cpd, cpd), :].reshape(cl, half).T

    for c in own[0] + own[1] + onward[0] + onward[1] + [tail_copy]:
        c.wait_send()
    await_all(fsend, f_sem.at[0])
    for h in range(2):
        await_all(vsend.at[h], v_send.at[h])
    await_all(csend, c_sem.at[0])
    await_all(gsend, g_sem.at[0])


def shards(n, yn, tokens, w_value, w_gate, short_value, short_gate, skip_bias, long_filter, grad_out):
    rows, dl = tokens.shape
    d, cl = w_value.shape
    half = rows // 2
    cpd = cl // n
    count = 2 * n
    taps = jnp.concatenate([short_value, short_gate], axis=0)
    consts = tables(n, half)
    block = (n, 2 * cpd, half)
    anywhere = pl.BlockSpec(memory_space=pl.ANY)
    vmem = pl.BlockSpec(memory_space=pltpu.VMEM)
    dma = pltpu.SemaphoreType.DMA
    scratch = [
        pltpu.VMEM((yn, rows, dl), BF16),
        pltpu.VMEM((d, 2 * cl), BF16),
        pltpu.VMEM((6, cl), F32),
        pltpu.VMEM((1, cl), F32),
        pltpu.VMEM((rows, cl), F32),
        pltpu.VMEM((rows, cl), BF16),
        *[pltpu.VMEM(c.shape, c.dtype) for c in consts],
        pltpu.VMEM((rows, 2 * cl), F32),
        pltpu.VMEM((HALO + rows, 2 * cl), F32),
        pltpu.VMEM((HALO, 2 * cl), BF16),
        pltpu.VMEM((HALO, 2 * cl), BF16),
        pltpu.VMEM((rows, cl), F32),
        pltpu.VMEM((rows, cl), F32),
        pltpu.VMEM(block, BF16),
        pltpu.VMEM(block, BF16),
        pltpu.VMEM((2, *block), BF16),
        pltpu.VMEM((2, *block), BF16),
        pltpu.VMEM(block, BF16),
        pltpu.VMEM(block, BF16),
        pltpu.VMEM(block, BF16),
        pltpu.VMEM(block, BF16),
        pltpu.VMEM(block, F32),
        pltpu.VMEM((2 * n * 2 * cpd, half), F32),
        pltpu.VMEM((cpd * count, 2 * half), BF16),
        pltpu.VMEM((cpd * count, 2 * half), F32),
        pltpu.VMEM((cpd * count, 2 * half), F32),
        pltpu.VMEM((cpd * count, 2 * half), F32),
        dma((10,)),
        dma((2 * yn,)),
        dma((8,)),
        dma((8,)),
        dma((2,)),
        dma((2,)),
        dma((2,)),
        dma((2,)),
        dma((2,)),
        dma((2,)),
    ]
    return pl.pallas_call(
        functools.partial(kernel, n, yn),
        out_shape=(
            jax.ShapeDtypeStruct((rows, cl), BF16),
            jax.ShapeDtypeStruct((rows, cl), F32),
        ),
        in_specs=[anywhere] * 12,
        out_specs=(vmem, vmem),
        scratch_shapes=scratch,
        compiler_params=pltpu.CompilerParams(
            collective_id=0, has_side_effects=True, vmem_limit_bytes=56 * 1024 * 1024
        ),
    )(tokens, w_value, w_gate, taps, skip_bias[None], long_filter, grad_out, *consts)


def solution(mesh):
    return jax.shard_map(
        functools.partial(shards, mesh.shape["seq"], mesh.shape["ch"]),
        mesh=mesh,
        in_specs=(
            P("seq", "ch"),
            P(None, "ch"),
            P(None, "ch"),
            P(None, "ch"),
            P(None, "ch"),
            P("ch"),
            P("seq", "ch"),
            P("seq", "ch"),
        ),
        out_specs=(P("seq", "ch"), P("seq", "ch")),
        check_vma=False,
    )
```

```python
import functools
import math

import jax
import jax.numpy as jnp
import numpy as np
from jax import lax
from jax.experimental import pallas as pl
from jax.experimental.pallas import tpu as pltpu
from jax.sharding import PartitionSpec as P

MESH = pl.DeviceIdType.MESH
F32 = jnp.float32
BF16 = jnp.bfloat16
HALO = 16


def tables(blocks, half):
    count = 2 * blocks
    row = np.arange(count)
    q = 2 * (row % blocks) + row // blocks
    k = np.arange(count)
    angle = 2 * np.pi * ((k[:, None] * q[None, :]) % count + q[None, :] / 4) / count
    first = np.concatenate([np.cos(angle), -np.sin(angle)], axis=0)
    last = np.concatenate([np.cos(angle).T, -np.sin(angle).T], axis=1) / (count * half)
    l = np.arange(half)
    twist = 2 * np.pi * (k[:, None] + 0.25) * l[None, :] / (count * half)
    turn = 2 * np.pi * ((l[:, None] * l[None, :]) % half) / half
    c, s = np.cos(turn), np.sin(turn)
    second = np.block([[c, -s], [s, c]])
    third = np.block([[c, s], [-s, c]])
    return (
        jnp.asarray(first, BF16),
        jnp.asarray(second, BF16),
        jnp.asarray(third, BF16),
        jnp.asarray(last, BF16),
        jnp.asarray(np.stack([np.cos(twist), np.sin(twist)]), F32),
    )


def dot(a, b):
    return jnp.dot(a, b, preferred_element_type=F32)


def transform_kernel(
    n, yn,
    tok_ref, wv_ref, wg_ref, taps_v_ref, taps_g_ref, skip_ref, filt_ref, gout_ref,
    first_ref, second_ref, third_ref, last_ref, twist_ref,
    crecv, grecv, gate_ref, base_ref,
    tok, wall, taps_v, taps_g, skip, filt, gout, first, second, third, last, twist,
    acc, proj, tail, tail_in, gate, base,
    fsend, frecv, asend, arecv, vsend, vrecv, msend, mrecv, csend, gsend,
    wide, fwide, awide, vwide, mwide, mid, spec_v, spec_h, spec_g,
    loc_sem, w_sem, ag_send, ag_recv, tail_sem, own_sem,
    f_sem, a_sem, v_sem, m_sem, c_sem, g_sem, met,
):
    seq = lax.axis_index("seq")
    ch = lax.axis_index("ch")
    rows, dl = tok_ref.shape
    cl = wv_ref.shape[1]
    half = rows // 2
    cpd = cl // n
    count = 2 * n
    group = 8 if n >= 32 else 1
    zs = n // group
    right, left = lax.rem(ch + 1, yn), lax.rem(ch + yn - 1, yn)
    far = lax.rem(ch + 2, yn)
    right_id, left_id = (seq, right), (seq, left)
    z, mate = seq // group, lax.rem(seq, group)

    def along_z(k):
        return (lax.rem(z + k + zs, zs) * group + mate, ch)

    def in_group(k):
        return (z * group + lax.rem(mate + k, group), ch)

    def local(i, src, dst):
        return pltpu.make_async_copy(src, dst, loc_sem.at[i])

    locals_ = [
        local(0, filt_ref, filt),
        local(1, tok_ref, tok.at[ch]),
        local(2, first_ref, first),
        local(3, second_ref, second),
        local(4, third_ref, third),
        local(5, last_ref, last),
        local(6, twist_ref, twist),
        local(7, taps_v_ref, taps_v),
        local(8, taps_g_ref, taps_g),
        local(9, skip_ref, skip),
        local(10, gout_ref, gout),
    ]

    def weight_copies(i, src):
        at = pl.ds(pl.multiple_of(src * dl, dl), dl)
        return [
            pltpu.make_async_copy(wv_ref.at[at], wall.at[at, pl.ds(0, cl)], w_sem.at[2 * i]),
            pltpu.make_async_copy(wg_ref.at[at], wall.at[at, pl.ds(cl, cl)], w_sem.at[2 * i + 1]),
        ]

    weights = [weight_copies(i, s) for i, s in enumerate((ch, left, right, far))]

    barrier = pltpu.get_barrier_semaphore()
    near = [right_id, left_id, along_z(1), along_z(-1)] + [in_group(k) for k in range(1, group)]
    for device in near:
        pl.semaphore_signal(barrier, inc=1, device_id=device, device_id_type=MESH)
    for c in locals_[:2] + weights[0] + locals_[2:]:
        c.start()
    for w in weights[1:]:
        for c in w:
            c.start()
    pl.semaphore_wait(barrier, len(near))

    cut = half - HALO
    spans = (pl.ds(cut, rows - cut), pl.ds(0, cut))

    def ag(i, src, dst, device):
        return pltpu.make_async_remote_copy(
            src_ref=src, dst_ref=dst, send_sem=ag_send.at[i], recv_sem=ag_recv.at[i],
            device_id=device, device_id_type=MESH,
        )

    own = [
        [ag(4 * p, tok_ref.at[spans[p]], tok.at[ch, spans[p]], right_id),
         ag(4 * p + 1, tok_ref.at[spans[p]], tok.at[ch, spans[p]], left_id)]
        for p in range(2)
    ]
    low, high = pl.ds(0, dl // 2), pl.ds(dl // 2, dl // 2)

    def forwards(p):
        a, b = tok.at[left, spans[p], low], tok.at[right, spans[p], high]
        return [ag(4 * p + 2, a, a, right_id), ag(4 * p + 3, b, b, left_id)]

    onward = [forwards(p) for p in range(2)]

    def from_neighbour(p, side):
        src = (left, right)[side]
        return ag(4 * p + side, tok.at[src, spans[p]], tok.at[src, spans[p]], (right_id, left_id)[side])

    def from_far(p, side):
        part = tok.at[far, spans[p], (low, high)[side]]
        return ag(4 * p + 2 + side, part, part, (right_id, left_id)[side])

    for c in own[0] + own[1]:
        c.start()

    def multiply(p, i, src, cols):
        part = dot(tok[src, spans[p], :], wall[pl.ds(pl.multiple_of(src * dl, dl), dl), cols])
        if i == 0:
            acc[spans[p], cols] = part
        else:
            acc[spans[p], cols] += part

    both = pl.ds(0, 2 * cl)

    rounds = [[along_z(1), along_z(-1)]]
    if zs > 4:
        rounds.append([along_z(2), along_z(-2)])
    if group > 1:
        rounds.append([in_group(k) for k in range(1, group)])

    def meet(r):
        for device in rounds[r]:
            pl.semaphore_signal(met.at[r], inc=1, device_id=device, device_id_type=MESH)

    def met_all(r):
        pl.semaphore_wait(met.at[r], len(rounds[r]))

    meet(0)
    locals_[0].wait()
    for h in range(2):
        turned = filt[pl.ds(h * half, half), :].T.reshape(n, cpd, half)
        wide[:, pl.ds(h * cpd, cpd), :] = turned
    fsend[...] = wide[...].astype(BF16)
    met_all(0)
    for r in range(1, len(rounds)):
        meet(r)
        if r == 1:
            locals_[1].wait()
            for c in weights[0]:
                c.wait()
            multiply(0, 0, ch, both)
        met_all(r)
    if len(rounds) < 2:
        locals_[1].wait()
        for c in weights[0]:
            c.wait()
        multiply(0, 0, ch, both)

    def scatter(src, dst, sem):
        def one(k, _):
            to = lax.rem(seq + k, n)
            pltpu.make_async_remote_copy(
                src_ref=src.at[to], dst_ref=dst.at[seq], send_sem=sem.at[0], recv_sem=sem.at[1],
                device_id=(to, ch), device_id_type=MESH,
            ).start()
            return 0

        lax.fori_loop(1, n, one, 0)

    def await_all(ref, sem):
        part = ref.at[pl.ds(0, n - 1)]
        pltpu.make_async_copy(part, part, sem).wait()

    scatter(fsend, frecv, f_sem)
    frecv[seq] = fsend[seq]
    multiply(1, 0, ch, both)

    for side in range(2):
        from_neighbour(0, side).wait_recv()
        onward[0][side].start()
    for w in weights[1:3]:
        for c in w:
            c.wait()
    multiply(0, 1, left, both)
    multiply(0, 2, right, both)
    for c in locals_[2:]:
        c.wait()

    tc, ts = twist[0], twist[1]

    def spectrum(load, spec):
        for pair in range(cpd // 2):
            c0, c1 = 2 * pair, 2 * pair + 1
            x = jnp.concatenate([load(c0), load(c1)], axis=1).astype(BF16)
            a = dot(first[...], x)
            for j, c in enumerate((c0, c1)):
                ar = a[:count, j * half:(j + 1) * half]
                ai = a[count:, j * half:(j + 1) * half]
                mid[pl.ds(c * count, count), pl.ds(0, half)] = (ar * tc + ai * ts).astype(BF16)
                mid[pl.ds(c * count, count), pl.ds(half, half)] = (ai * tc - ar * ts).astype(BF16)
        spec[...] = dot(mid[...], second[...])

    def restore(pr, pi, send):
        mid[:, pl.ds(0, half)] = pr.astype(BF16)
        mid[:, pl.ds(half, half)] = pi.astype(BF16)
        spec_g[...] = dot(mid[...], third[...])
        for pair in range(cpd // 2):
            two = []
            for c in (2 * pair, 2 * pair + 1):
                zr = spec_g[pl.ds(c * count, count), pl.ds(0, half)]
                zi = spec_g[pl.ds(c * count, count), pl.ds(half, half)]
                two.append(jnp.concatenate([zr * tc - zi * ts, zi * tc + zr * ts], axis=0).astype(BF16))
            y = dot(last[...], jnp.concatenate(two, axis=1))
            for j in range(2):
                for h in range(2):
                    fwide[pl.ds(h * cpd + 2 * pair + j, n, stride=2 * cpd), :] = (
                        y[h * n:(h + 1) * n, j * half:(j + 1) * half])
        send[...] = fwide[...].astype(BF16).reshape(n, 2 * cpd, half)

    def rows_of(low_ref, low_at, low_stride, high_ref, high_at, high_stride):
        return lambda c: jnp.concatenate(
            [low_ref[pl.ds(low_at + c, n, stride=low_stride), :],
             high_ref[pl.ds(high_at + c, n, stride=high_stride), :]], axis=0)

    await_all(frecv, f_sem.at[1])
    fwide[...] = frecv[...].astype(F32).reshape(n * 2 * cpd, half)
    spectrum(rows_of(fwide, 0, 2 * cpd, fwide, cpd, 2 * cpd), spec_h)

    def short(h, taps, col):
        cols = pl.ds(col, cl)
        return (
            taps[0:1, :] * proj[pl.ds(HALO + h * half, half), cols]
            + taps[1:2, :] * proj[pl.ds(HALO - 1 + h * half, half), cols]
            + taps[2:3, :] * proj[pl.ds(HALO - 2 + h * half, half), cols]
        )

    def finish(p, cols):
        proj[pl.ds(spans[p].start + HALO, spans[p].size), cols] = acc[spans[p], cols].astype(BF16).astype(F32)

    def gated(h, v):
        at = pl.ds(h * half, half)
        g = short(h, taps_g, cl)
        gate[at, :] = g
        base[at, :] = g * skip[...] * v
        return gout[at, :].astype(F32) * g

    for side in range(2):
        from_neighbour(1, side).wait_recv()
        onward[1][side].start()

    for side in range(2):
        from_far(0, side).wait_recv()
    for c in weights[3]:
        c.wait()
    multiply(0, 3, far, both)
    finish(0, both)
    tail[...] = proj[pl.ds(rows, HALO), :].astype(BF16)
    tail_copy = pltpu.make_async_remote_copy(
        src_ref=tail, dst_ref=tail_in, send_sem=tail_sem.at[0], recv_sem=tail_sem.at[1],
        device_id=(lax.rem(seq + 1, n), ch), device_id_type=MESH,
    )
    tail_copy.start()
    v = short(1, taps_v, 0)
    mixed = gated(1, v)
    asend[...] = jnp.concatenate(
        [v.T.reshape(n, cpd, half), mixed.T.reshape(n, cpd, half)], axis=1).astype(BF16)
    scatter(asend, arecv, a_sem)
    arecv[seq] = asend[seq]

    multiply(1, 1, left, both)
    multiply(1, 2, right, both)
    tail_copy.wait_recv()
    proj[pl.ds(0, HALO), :] = jnp.where(seq > 0, tail_in[...].astype(F32), 0.0)
    value_cols, gate_cols = pl.ds(0, cl), pl.ds(cl, cl)
    for side in range(2):
        from_far(1, side).wait_recv()
    multiply(1, 3, far, value_cols)
    finish(1, value_cols)
    v = short(0, taps_v, 0)
    vsend[...] = v.T.reshape(n, cpd, half).astype(BF16)
    scatter(vsend, vrecv, v_sem)
    vrecv[seq] = vsend[seq]
    multiply(1, 3, far, gate_cols)
    finish(1, gate_cols)
    mixed = gated(0, v)
    msend[...] = mixed.T.reshape(n, cpd, half).astype(BF16)
    scatter(msend, mrecv, m_sem)
    mrecv[seq] = msend[seq]
    results = [local(0, gate, gate_ref), local(1, base, base_ref)]
    for c in results:
        c.start()

    await_all(arecv, a_sem.at[1])
    awide[...] = arecv[...].astype(F32).reshape(n * 2 * cpd, half)
    await_all(vrecv, v_sem.at[1])
    vwide[...] = vrecv[...].astype(F32).reshape(n * cpd, half)
    spectrum(rows_of(vwide, 0, cpd, awide, 0, 2 * cpd), spec_v)
    re, im = pl.ds(0, half), pl.ds(half, half)
    vr, vi = spec_v[:, re], spec_v[:, im]
    hr, hi = spec_h[:, re], spec_h[:, im]
    restore(vr * hr - vi * hi, vr * hi + vi * hr, csend)
    scatter(csend, crecv, c_sem)
    stays = [pltpu.make_async_copy(csend.at[seq], crecv.at[seq], own_sem.at[0])]
    stays[0].start()

    await_all(mrecv, m_sem.at[1])
    mwide[...] = mrecv[...].astype(F32).reshape(n * cpd, half)
    spectrum(rows_of(mwide, 0, cpd, awide, cpd, 2 * cpd), spec_g)
    gr, gi = spec_g[:, re], spec_g[:, im]
    vr, vi = spec_v[:, re], spec_v[:, im]
    restore(gr * vr + gi * vi, gi * vr - gr * vi, gsend)
    scatter(gsend, grecv, g_sem)
    stays.append(pltpu.make_async_copy(gsend.at[seq], grecv.at[seq], own_sem.at[1]))
    stays[1].start()

    for c in own[0] + own[1] + onward[0] + onward[1] + [tail_copy]:
        c.wait_send()
    for c in results + stays:
        c.wait()
    for ref, sem in ((fsend, f_sem), (asend, a_sem), (vsend, v_sem), (msend, m_sem)):
        await_all(ref, sem.at[0])
    await_all(crecv, c_sem.at[1])
    await_all(csend, c_sem.at[0])
    await_all(grecv, g_sem.at[1])
    await_all(gsend, g_sem.at[0])


def closing_kernel(conv_ref, grad_ref, gate_ref, base_ref, out_ref, fgrad_ref):
    cpd = conv_ref.shape[1] // 2
    half = conv_ref.shape[2]
    columns = out_ref.shape[1]

    def turned(ref, h):
        return ref[...].astype(F32)[:, h * cpd:(h + 1) * cpd, :].reshape(columns, half).T

    for h in range(2):
        at = pl.ds(h * half, half)
        out_ref[at, :] = (gate_ref[at, :] * turned(conv_ref, h) + base_ref[at, :]).astype(BF16)
        fgrad_ref[at, :] = turned(grad_ref, h)


def shards(n, yn, tokens, w_value, w_gate, short_value, short_gate, skip_bias, long_filter, grad_out):
    rows, dl = tokens.shape
    d, cl = w_value.shape
    half = rows // 2
    cpd = cl // n
    count = 2 * n
    consts = tables(n, half)
    block = (n, 2 * cpd, half)
    small = (n, cpd, half)
    anywhere = pl.BlockSpec(memory_space=pl.ANY)
    dma = pltpu.SemaphoreType.DMA
    scratch = [
        pltpu.VMEM((yn, rows, dl), BF16),
        pltpu.VMEM((d, 2 * cl), BF16),
        pltpu.VMEM((3, cl), F32),
        pltpu.VMEM((3, cl), F32),
        pltpu.VMEM((1, cl), F32),
        pltpu.VMEM((rows, cl), F32),
        pltpu.VMEM((rows, cl), BF16),
        *[pltpu.VMEM(c.shape, c.dtype) for c in consts],
        pltpu.VMEM((rows, 2 * cl), F32),
        pltpu.VMEM((HALO + rows, 2 * cl), F32),
        pltpu.VMEM((HALO, 2 * cl), BF16),
        pltpu.VMEM((HALO, 2 * cl), BF16),
        pltpu.VMEM((rows, cl), F32),
        pltpu.VMEM((rows, cl), F32),
        pltpu.VMEM(block, BF16),
        pltpu.VMEM(block, BF16),
        pltpu.VMEM(block, BF16),
        pltpu.VMEM(block, BF16),
        pltpu.VMEM(small, BF16),
        pltpu.VMEM(small, BF16),
        pltpu.VMEM(small, BF16),
        pltpu.VMEM(small, BF16),
        pltpu.VMEM(block, BF16),
        pltpu.VMEM(block, BF16),
        pltpu.VMEM(block, F32),
        pltpu.VMEM((n * 2 * cpd, half), F32),
        pltpu.VMEM((n * 2 * cpd, half), F32),
        pltpu.VMEM((n * cpd, half), F32),
        pltpu.VMEM((n * cpd, half), F32),
        pltpu.VMEM((cpd * count, 2 * half), BF16),
        pltpu.VMEM((cpd * count, 2 * half), F32),
        pltpu.VMEM((cpd * count, 2 * half), F32),
        pltpu.VMEM((cpd * count, 2 * half), F32),
        dma((11,)),
        dma((2 * yn,)),
        dma((8,)),
        dma((8,)),
        dma((2,)),
        dma((2,)),
        dma((2,)),
        dma((2,)),
        dma((2,)),
        dma((2,)),
        dma((2,)),
        dma((2,)),
        pltpu.SemaphoreType.REGULAR((3,)),
    ]
    conv, grad, gate, base = pl.pallas_call(
        functools.partial(transform_kernel, n, yn),
        out_shape=(
            jax.ShapeDtypeStruct(block, BF16),
            jax.ShapeDtypeStruct(block, BF16),
            jax.ShapeDtypeStruct((rows, cl), F32),
            jax.ShapeDtypeStruct((rows, cl), F32),
        ),
        in_specs=[anywhere] * 13,
        out_specs=[anywhere] * 4,
        scratch_shapes=scratch,
        compiler_params=pltpu.CompilerParams(
            collective_id=0, has_side_effects=True, vmem_limit_bytes=56 * 1024 * 1024
        ),
    )(tokens, w_value, w_gate, short_value, short_gate, skip_bias[None], long_filter, grad_out, *consts)
    steps = 2
    blocks = pl.BlockSpec((n // steps, 2 * cpd, half), lambda i: (i, 0, 0))
    columns = pl.BlockSpec((rows, cl // steps), lambda i: (0, i))
    return pl.pallas_call(
        closing_kernel,
        grid=(steps,),
        out_shape=(
            jax.ShapeDtypeStruct((rows, cl), BF16),
            jax.ShapeDtypeStruct((rows, cl), F32),
        ),
        in_specs=[blocks, blocks, columns, columns],
        out_specs=(columns, columns),
    )(conv, grad, gate, base)


def solution(mesh):
    return jax.shard_map(
        functools.partial(shards, mesh.shape["seq"], mesh.shape["ch"]),
        mesh=mesh,
        in_specs=(
            P("seq", "ch"),
            P(None, "ch"),
            P(None, "ch"),
            P(None, "ch"),
            P(None, "ch"),
            P("ch"),
            P("seq", "ch"),
            P("seq", "ch"),
        ),
        out_specs=(P("seq", "ch"), P("seq", "ch")),
        check_vma=False,
    )
```

```python
import functools
import math

import jax
import jax.numpy as jnp
import numpy as np
from jax import lax
from jax.experimental import pallas as pl
from jax.experimental.pallas import tpu as pltpu
from jax.sharding import PartitionSpec as P

MESH = pl.DeviceIdType.MESH
F32 = jnp.float32
BF16 = jnp.bfloat16
HALO = 16


def tables(blocks, half):
    count = 2 * blocks
    row = np.arange(count)
    q = 2 * (row % blocks) + row // blocks
    k = np.arange(count)
    angle = 2 * np.pi * ((k[:, None] * q[None, :]) % count + q[None, :] / 4) / count
    first = np.concatenate([np.cos(angle), -np.sin(angle)], axis=0)
    last = np.concatenate([np.cos(angle).T, -np.sin(angle).T], axis=1) / (count * half)
    l = np.arange(half)
    twist = 2 * np.pi * (k[:, None] + 0.25) * l[None, :] / (count * half)
    turn = 2 * np.pi * ((l[:, None] * l[None, :]) % half) / half
    c, s = np.cos(turn), np.sin(turn)
    second = np.block([[c, -s], [s, c]])
    third = np.block([[c, s], [-s, c]])
    return (
        jnp.asarray(first, BF16),
        jnp.asarray(second, BF16),
        jnp.asarray(third, BF16),
        jnp.asarray(last, BF16),
        jnp.asarray(np.stack([np.cos(twist), np.sin(twist)]), F32),
    )


def dot(a, b):
    return jnp.dot(a, b, preferred_element_type=F32)


def transform_kernel(
    n, yn,
    tok_ref, wv_ref, wg_ref, taps_v_ref, taps_g_ref, skip_ref, filt_ref, gout_ref,
    first_ref, second_ref, third_ref, last_ref, twist_ref,
    crecv, grecv, gate_ref, base_ref,
    tok, wall, taps_v, taps_g, skip, filt, gout, first, second, third, last, twist,
    acc, proj, tail, tail_in, gate, base,
    fsend, frecv, vsend, vrecv, msend, mrecv, csend, gsend,
    wide, fwide, vwide, mid, spec_v, spec_h, spec_g,
    loc_sem, w_sem, ag_send, ag_recv, tail_sem, own_sem,
    f_sem, v_sem, m_sem, c_sem, g_sem, met,
):
    seq = lax.axis_index("seq")
    ch = lax.axis_index("ch")
    rows, dl = tok_ref.shape
    cl = wv_ref.shape[1]
    half = rows // 2
    cpd = cl // n
    count = 2 * n
    group = 8 if n >= 32 else 1
    zs = n // group
    right, left = lax.rem(ch + 1, yn), lax.rem(ch + yn - 1, yn)
    far = lax.rem(ch + 2, yn)
    right_id, left_id = (seq, right), (seq, left)
    z, mate = seq // group, lax.rem(seq, group)

    def along_z(k):
        return (lax.rem(z + k + zs, zs) * group + mate, ch)

    def in_group(k):
        return (z * group + lax.rem(mate + k, group), ch)

    def local(i, src, dst):
        return pltpu.make_async_copy(src, dst, loc_sem.at[i])

    locals_ = [
        local(0, filt_ref, filt),
        local(1, tok_ref, tok.at[ch]),
        local(2, first_ref, first),
        local(3, second_ref, second),
        local(4, third_ref, third),
        local(5, last_ref, last),
        local(6, twist_ref, twist),
        local(7, taps_v_ref, taps_v),
        local(8, taps_g_ref, taps_g),
        local(9, skip_ref, skip),
        local(10, gout_ref, gout),
    ]

    def weight_copies(i, src):
        at = pl.ds(pl.multiple_of(src * dl, dl), dl)
        return [
            pltpu.make_async_copy(wv_ref.at[at], wall.at[at, pl.ds(0, cl)], w_sem.at[2 * i]),
            pltpu.make_async_copy(wg_ref.at[at], wall.at[at, pl.ds(cl, cl)], w_sem.at[2 * i + 1]),
        ]

    weights = [weight_copies(i, s) for i, s in enumerate((ch, left, right, far))]

    barrier = pltpu.get_barrier_semaphore()
    near = [right_id, left_id, along_z(1), along_z(-1)] + [in_group(k) for k in range(1, group)]
    for device in near:
        pl.semaphore_signal(barrier, inc=1, device_id=device, device_id_type=MESH)
    for c in locals_:
        c.start()
    for w in weights:
        for c in w:
            c.start()
    pl.semaphore_wait(barrier, len(near))

    cut = half - HALO
    spans = (pl.ds(cut, rows - cut), pl.ds(0, cut))
    pieces = spans

    def ag(i, src, dst, device):
        return pltpu.make_async_remote_copy(
            src_ref=src, dst_ref=dst, send_sem=ag_send.at[i], recv_sem=ag_recv.at[i],
            device_id=device, device_id_type=MESH,
        )

    own = [
        [ag(4 * p, tok_ref.at[at], tok.at[ch, at], right_id),
         ag(4 * p + 1, tok_ref.at[at], tok.at[ch, at], left_id)]
        for p, at in enumerate(pieces)
    ]
    low, high = pl.ds(0, dl // 2), pl.ds(dl // 2, dl // 2)

    def forwards(p):
        a, b = tok.at[left, pieces[p], low], tok.at[right, pieces[p], high]
        return [ag(4 * p + 2, a, a, right_id), ag(4 * p + 3, b, b, left_id)]

    onward = [forwards(p) for p in range(len(pieces))]

    def from_neighbour(p, side):
        src = (left, right)[side]
        part = tok.at[src, pieces[p]]
        return ag(4 * p + side, part, part, (right_id, left_id)[side])

    def from_far(p, side):
        part = tok.at[far, pieces[p], (low, high)[side]]
        return ag(4 * p + 2 + side, part, part, (right_id, left_id)[side])

    for c in own[0] + own[1]:
        c.start()

    def multiply(p, i, src, cols):
        part = dot(tok[src, spans[p], :], wall[pl.ds(pl.multiple_of(src * dl, dl), dl), cols])
        if i == 0:
            acc[spans[p], cols] = part
        else:
            acc[spans[p], cols] += part

    both = pl.ds(0, 2 * cl)

    rounds = [[along_z(1), along_z(-1)]]
    if zs > 4:
        rounds.append([along_z(2), along_z(-2)])
    if group > 1:
        rounds.append([in_group(k) for k in range(1, group)])

    def meet(r):
        for device in rounds[r]:
            pl.semaphore_signal(met.at[r], inc=1, device_id=device, device_id_type=MESH)

    def met_all(r):
        pl.semaphore_wait(met.at[r], len(rounds[r]))

    meet(0)
    locals_[0].wait()
    for h in range(2):
        turned = filt[pl.ds(h * half, half), :].T.reshape(n, cpd, half)
        wide[:, pl.ds(h * cpd, cpd), :] = turned
    fsend[...] = wide[...].astype(BF16)
    met_all(0)
    for r in range(1, len(rounds)):
        meet(r)
        if r == 1:
            locals_[1].wait()
            for c in weights[0]:
                c.wait()
            multiply(0, 0, ch, both)
        met_all(r)
    if len(rounds) < 2:
        locals_[1].wait()
        for c in weights[0]:
            c.wait()
        multiply(0, 0, ch, both)

    def scatter(src, dst, sem):
        def one(k, _):
            j, r = lax.rem(k, zs), group - 1 - k // zs
            odd = lax.rem(j, 2)
            dz = zs // 2 + (j // 2) * (1 - odd) - ((j + 1) // 2) * odd
            x = lax.rem(mate // 2 + r // 2, max(group // 2, 1))
            to = lax.rem(z + dz, zs) * group + x * 2 + lax.rem(mate + r, min(group, 2))
            pltpu.make_async_remote_copy(
                src_ref=src.at[to], dst_ref=dst.at[seq], send_sem=sem.at[0], recv_sem=sem.at[1],
                device_id=(to, ch), device_id_type=MESH,
            ).start()
            return 0

        lax.fori_loop(0, n - 1, one, 0)

    def await_all(ref, sem):
        part = ref.at[pl.ds(0, n - 1)]
        pltpu.make_async_copy(part, part, sem).wait()

    scatter(fsend, frecv, f_sem)
    frecv[seq] = fsend[seq]
    multiply(1, 0, ch, both)

    def pass_on(p):
        for side in range(2):
            from_neighbour(p, side).wait_recv()
            onward[p][side].start()

    pass_on(0)
    for w in weights[1:3]:
        for c in w:
            c.wait()
    multiply(0, 1, left, both)
    multiply(0, 2, right, both)
    for c in locals_[2:]:
        c.wait()

    tc, ts = twist[0], twist[1]

    def spectrum(load, spec):
        for pair in range(cpd // 2):
            c0, c1 = 2 * pair, 2 * pair + 1
            x = jnp.concatenate([load(c0), load(c1)], axis=1).astype(BF16)
            a = dot(first[...], x)
            for j, c in enumerate((c0, c1)):
                ar = a[:count, j * half:(j + 1) * half]
                ai = a[count:, j * half:(j + 1) * half]
                mid[pl.ds(c * count, count), pl.ds(0, half)] = (ar * tc + ai * ts).astype(BF16)
                mid[pl.ds(c * count, count), pl.ds(half, half)] = (ai * tc - ar * ts).astype(BF16)
        spec[...] = dot(mid[...], second[...])

    def restore(pr, pi, send):
        mid[:, pl.ds(0, half)] = pr.astype(BF16)
        mid[:, pl.ds(half, half)] = pi.astype(BF16)
        spec_g[...] = dot(mid[...], third[...])
        for pair in range(cpd // 2):
            two = []
            for c in (2 * pair, 2 * pair + 1):
                zr = spec_g[pl.ds(c * count, count), pl.ds(0, half)]
                zi = spec_g[pl.ds(c * count, count), pl.ds(half, half)]
                two.append(jnp.concatenate([zr * tc - zi * ts, zi * tc + zr * ts], axis=0).astype(BF16))
            y = dot(last[...], jnp.concatenate(two, axis=1))
            for j in range(2):
                for h in range(2):
                    fwide[pl.ds(h * cpd + 2 * pair + j, n, stride=2 * cpd), :] = (
                        y[h * n:(h + 1) * n, j * half:(j + 1) * half])
        send[...] = fwide[...].astype(BF16).reshape(n, 2 * cpd, half)

    def rows_of(low_ref, low_at, low_stride, high_ref, high_at, high_stride):
        return lambda c: jnp.concatenate(
            [low_ref[pl.ds(low_at + c, n, stride=low_stride), :],
             high_ref[pl.ds(high_at + c, n, stride=high_stride), :]], axis=0)


    def short(h, taps, col):
        cols = pl.ds(col, cl)
        return (
            taps[0:1, :] * proj[pl.ds(HALO + h * half, half), cols]
            + taps[1:2, :] * proj[pl.ds(HALO - 1 + h * half, half), cols]
            + taps[2:3, :] * proj[pl.ds(HALO - 2 + h * half, half), cols]
        )

    def finish(p, cols):
        proj[pl.ds(spans[p].start + HALO, spans[p].size), cols] = acc[spans[p], cols].astype(BF16).astype(F32)

    def gated(h, v):
        at = pl.ds(h * half, half)
        g = short(h, taps_g, cl)
        gate[at, :] = g
        base[at, :] = g * skip[...] * v
        return gout[at, :].astype(F32) * g

    for p in range(1, len(pieces)):
        pass_on(p)

    for side in range(2):
        from_far(0, side).wait_recv()
    for c in weights[3]:
        c.wait()
    multiply(0, 3, far, both)
    finish(0, both)
    tail[...] = proj[pl.ds(rows, HALO), :].astype(BF16)
    tail_copy = pltpu.make_async_remote_copy(
        src_ref=tail, dst_ref=tail_in, send_sem=tail_sem.at[0], recv_sem=tail_sem.at[1],
        device_id=(lax.rem(seq + 1, n), ch), device_id_type=MESH,
    )
    tail_copy.start()
    v = short(1, taps_v, 0)
    vsend[1] = v.T.reshape(n, cpd, half).astype(BF16)
    scatter(vsend.at[1], vrecv.at[1], v_sem.at[1])
    vrecv[1, seq] = vsend[1, seq]
    msend[1] = gated(1, v).T.reshape(n, cpd, half).astype(BF16)
    mrecv[1, seq] = msend[1, seq]

    await_all(frecv, f_sem.at[1])
    fwide[...] = frecv[...].astype(F32).reshape(n * 2 * cpd, half)
    spectrum(rows_of(fwide, 0, 2 * cpd, fwide, cpd, 2 * cpd), spec_h)

    multiply(1, 1, left, both)
    multiply(1, 2, right, both)
    tail_copy.wait_recv()
    proj[pl.ds(0, HALO), :] = jnp.where(seq > 0, tail_in[...].astype(F32), 0.0)
    value_cols, gate_cols = pl.ds(0, cl), pl.ds(cl, cl)
    for p in range(1, len(pieces)):
        for side in range(2):
            from_far(p, side).wait_recv()
    multiply(1, 3, far, value_cols)
    finish(1, value_cols)
    v = short(0, taps_v, 0)
    vsend[0] = v.T.reshape(n, cpd, half).astype(BF16)
    scatter(vsend.at[0], vrecv.at[0], v_sem.at[0])
    vrecv[0, seq] = vsend[0, seq]
    scatter(msend.at[1], mrecv.at[1], m_sem.at[1])
    multiply(1, 3, far, gate_cols)
    finish(1, gate_cols)
    msend[0] = gated(0, v).T.reshape(n, cpd, half).astype(BF16)
    scatter(msend.at[0], mrecv.at[0], m_sem.at[0])
    mrecv[0, seq] = msend[0, seq]
    results = [local(0, gate, gate_ref), local(1, base, base_ref)]
    for c in results:
        c.start()

    for h in (1, 0):
        await_all(vrecv.at[h], v_sem.at[h, 1])
        vwide[h] = vrecv[h].astype(F32).reshape(n * cpd, half)
    spectrum(rows_of(vwide.at[0], 0, cpd, vwide.at[1], 0, cpd), spec_v)
    re, im = pl.ds(0, half), pl.ds(half, half)
    vr, vi = spec_v[:, re], spec_v[:, im]
    hr, hi = spec_h[:, re], spec_h[:, im]
    restore(vr * hr - vi * hi, vr * hi + vi * hr, csend)
    scatter(csend, crecv, c_sem)
    stays = [pltpu.make_async_copy(csend.at[seq], crecv.at[seq], own_sem.at[0])]
    stays[0].start()

    for h in (1, 0):
        await_all(mrecv.at[h], m_sem.at[h, 1])
        vwide[h] = mrecv[h].astype(F32).reshape(n * cpd, half)
    spectrum(rows_of(vwide.at[0], 0, cpd, vwide.at[1], 0, cpd), spec_g)
    gr, gi = spec_g[:, re], spec_g[:, im]
    vr, vi = spec_v[:, re], spec_v[:, im]
    restore(gr * vr + gi * vi, gi * vr - gr * vi, gsend)
    scatter(gsend, grecv, g_sem)
    stays.append(pltpu.make_async_copy(gsend.at[seq], grecv.at[seq], own_sem.at[1]))
    stays[1].start()

    for c in sum(own + onward, [tail_copy]):
        c.wait_send()
    for c in results + stays:
        c.wait()
    await_all(fsend, f_sem.at[0])
    for h in range(2):
        await_all(vsend.at[h], v_sem.at[h, 0])
        await_all(msend.at[h], m_sem.at[h, 0])
    await_all(crecv, c_sem.at[1])
    await_all(csend, c_sem.at[0])
    await_all(grecv, g_sem.at[1])
    await_all(gsend, g_sem.at[0])


def closing_kernel(conv_ref, grad_ref, gate_ref, base_ref, out_ref, fgrad_ref):
    cpd = conv_ref.shape[1] // 2
    half = conv_ref.shape[2]
    columns = out_ref.shape[1]

    def turned(ref, h):
        return ref[...].astype(F32)[:, h * cpd:(h + 1) * cpd, :].reshape(columns, half).T

    for h in range(2):
        at = pl.ds(h * half, half)
        out_ref[at, :] = (gate_ref[at, :] * turned(conv_ref, h) + base_ref[at, :]).astype(BF16)
        fgrad_ref[at, :] = turned(grad_ref, h)


def shards(n, yn, tokens, w_value, w_gate, short_value, short_gate, skip_bias, long_filter, grad_out):
    rows, dl = tokens.shape
    d, cl = w_value.shape
    half = rows // 2
    cpd = cl // n
    count = 2 * n
    consts = tables(n, half)
    block = (n, 2 * cpd, half)
    small = (n, cpd, half)
    anywhere = pl.BlockSpec(memory_space=pl.ANY)
    dma = pltpu.SemaphoreType.DMA
    scratch = [
        pltpu.VMEM((yn, rows, dl), BF16),
        pltpu.VMEM((d, 2 * cl), BF16),
        pltpu.VMEM((3, cl), F32),
        pltpu.VMEM((3, cl), F32),
        pltpu.VMEM((1, cl), F32),
        pltpu.VMEM((rows, cl), F32),
        pltpu.VMEM((rows, cl), BF16),
        *[pltpu.VMEM(c.shape, c.dtype) for c in consts],
        pltpu.VMEM((rows, 2 * cl), F32),
        pltpu.VMEM((HALO + rows, 2 * cl), F32),
        pltpu.VMEM((HALO, 2 * cl), BF16),
        pltpu.VMEM((HALO, 2 * cl), BF16),
        pltpu.VMEM((rows, cl), F32),
        pltpu.VMEM((rows, cl), F32),
        pltpu.VMEM(block, BF16),
        pltpu.VMEM(block, BF16),
        pltpu.VMEM((2, *small), BF16),
        pltpu.VMEM((2, *small), BF16),
        pltpu.VMEM((2, *small), BF16),
        pltpu.VMEM((2, *small), BF16),
        pltpu.VMEM(block, BF16),
        pltpu.VMEM(block, BF16),
        pltpu.VMEM(block, F32),
        pltpu.VMEM((n * 2 * cpd, half), F32),
        pltpu.VMEM((2, n * cpd, half), F32),
        pltpu.VMEM((cpd * count, 2 * half), BF16),
        pltpu.VMEM((cpd * count, 2 * half), F32),
        pltpu.VMEM((cpd * count, 2 * half), F32),
        pltpu.VMEM((cpd * count, 2 * half), F32),
        dma((11,)),
        dma((2 * yn,)),
        dma((12,)),
        dma((12,)),
        dma((2,)),
        dma((2,)),
        dma((2,)),
        dma((2, 2)),
        dma((2, 2)),
        dma((2,)),
        dma((2,)),
        pltpu.SemaphoreType.REGULAR((3,)),
    ]
    conv, grad, gate, base = pl.pallas_call(
        functools.partial(transform_kernel, n, yn),
        out_shape=(
            jax.ShapeDtypeStruct(block, BF16),
            jax.ShapeDtypeStruct(block, BF16),
            jax.ShapeDtypeStruct((rows, cl), F32),
            jax.ShapeDtypeStruct((rows, cl), F32),
        ),
        in_specs=[anywhere] * 13,
        out_specs=[anywhere] * 4,
        scratch_shapes=scratch,
        compiler_params=pltpu.CompilerParams(
            collective_id=0, has_side_effects=True, vmem_limit_bytes=56 * 1024 * 1024
        ),
    )(tokens, w_value, w_gate, short_value, short_gate, skip_bias[None], long_filter, grad_out, *consts)
    steps = 2
    blocks = pl.BlockSpec((n // steps, 2 * cpd, half), lambda i: (i, 0, 0))
    columns = pl.BlockSpec((rows, cl // steps), lambda i: (0, i))
    return pl.pallas_call(
        closing_kernel,
        grid=(steps,),
        out_shape=(
            jax.ShapeDtypeStruct((rows, cl), BF16),
            jax.ShapeDtypeStruct((rows, cl), F32),
        ),
        in_specs=[blocks, blocks, columns, columns],
        out_specs=(columns, columns),
    )(conv, grad, gate, base)


def solution(mesh):
    return jax.shard_map(
        functools.partial(shards, mesh.shape["seq"], mesh.shape["ch"]),
        mesh=mesh,
        in_specs=(
            P("seq", "ch"),
            P(None, "ch"),
            P(None, "ch"),
            P(None, "ch"),
            P(None, "ch"),
            P("ch"),
            P("seq", "ch"),
            P("seq", "ch"),
        ),
        out_specs=(P("seq", "ch"), P("seq", "ch")),
        check_vma=False,
    )
```

```python
import functools
import math

import jax
import jax.numpy as jnp
import numpy as np
from jax import lax
from jax.experimental import pallas as pl
from jax.experimental.pallas import tpu as pltpu
from jax.sharding import PartitionSpec as P

MESH = pl.DeviceIdType.MESH
F32 = jnp.float32
BF16 = jnp.bfloat16
HALO = 16


def tables(blocks, half):
    count = 2 * blocks
    row = np.arange(count)
    q = 2 * (row % blocks) + row // blocks
    k = np.arange(count)
    angle = 2 * np.pi * ((k[:, None] * q[None, :]) % count + q[None, :] / 4) / count
    first = np.concatenate([np.cos(angle), -np.sin(angle)], axis=0)
    last = np.concatenate([np.cos(angle).T, -np.sin(angle).T], axis=1) / (count * half)
    l = np.arange(half)
    twist = 2 * np.pi * (k[:, None] + 0.25) * l[None, :] / (count * half)
    turn = 2 * np.pi * ((l[:, None] * l[None, :]) % half) / half
    c, s = np.cos(turn), np.sin(turn)
    second = np.block([[c, -s], [s, c]])
    third = np.block([[c, s], [-s, c]])
    return (
        jnp.asarray(first, BF16),
        jnp.asarray(second, BF16),
        jnp.asarray(third, BF16),
        jnp.asarray(last, BF16),
        jnp.asarray(np.stack([np.cos(twist), np.sin(twist)]), F32),
    )


def dot(a, b):
    return jnp.dot(a, b, preferred_element_type=F32)


def transform_kernel(
    n, yn,
    tok_ref, wv_ref, wg_ref, taps_v_ref, taps_g_ref, skip_ref, filt_ref, gout_ref,
    first_ref, second_ref, third_ref, last_ref, twist_ref,
    grecv, out_ref,
    tok, wall, taps_v, taps_g, skip, filt, gout, first, second, third, last, twist,
    acc, proj, tail, tail_in, gate, base,
    fsend, frecv, vsend, vrecv, msend, mrecv, csend, crecv, gsend, out,
    wide, fwide, vwide, mid, spec_v, spec_h, spec_g,
    loc_sem, w_sem, ag_send, ag_recv, tail_sem, own_sem,
    f_sem, v_sem, m_sem, c_sem, g_sem, met,
):
    seq = lax.axis_index("seq")
    ch = lax.axis_index("ch")
    rows, dl = tok_ref.shape
    cl = wv_ref.shape[1]
    half = rows // 2
    cpd = cl // n
    count = 2 * n
    group = 8 if n >= 32 else 1
    zs = n // group
    right, left = lax.rem(ch + 1, yn), lax.rem(ch + yn - 1, yn)
    far = lax.rem(ch + 2, yn)
    right_id, left_id = (seq, right), (seq, left)
    z, mate = seq // group, lax.rem(seq, group)

    def along_z(k):
        return (lax.rem(z + k + zs, zs) * group + mate, ch)

    def in_group(k):
        return (z * group + lax.rem(mate + k, group), ch)

    def local(i, src, dst):
        return pltpu.make_async_copy(src, dst, loc_sem.at[i])

    locals_ = [
        local(0, filt_ref, filt),
        local(1, tok_ref, tok.at[ch]),
        local(2, first_ref, first),
        local(3, second_ref, second),
        local(4, third_ref, third),
        local(5, last_ref, last),
        local(6, twist_ref, twist),
        local(7, taps_v_ref, taps_v),
        local(8, taps_g_ref, taps_g),
        local(9, skip_ref, skip),
        local(10, gout_ref, gout),
    ]

    def weight_copies(i, src):
        at = pl.ds(pl.multiple_of(src * dl, dl), dl)
        return [
            pltpu.make_async_copy(wv_ref.at[at], wall.at[at, pl.ds(0, cl)], w_sem.at[2 * i]),
            pltpu.make_async_copy(wg_ref.at[at], wall.at[at, pl.ds(cl, cl)], w_sem.at[2 * i + 1]),
        ]

    weights = [weight_copies(i, s) for i, s in enumerate((ch, left, right, far))]

    barrier = pltpu.get_barrier_semaphore()
    near = [right_id, left_id, along_z(1), along_z(-1)] + [in_group(k) for k in range(1, group)]
    for device in near:
        pl.semaphore_signal(barrier, inc=1, device_id=device, device_id_type=MESH)
    for c in locals_:
        c.start()
    for w in weights:
        for c in w:
            c.start()
    pl.semaphore_wait(barrier, len(near))

    cut = half - HALO
    spans = (pl.ds(cut, rows - cut), pl.ds(0, cut))
    pieces = spans

    def ag(i, src, dst, device):
        return pltpu.make_async_remote_copy(
            src_ref=src, dst_ref=dst, send_sem=ag_send.at[i], recv_sem=ag_recv.at[i],
            device_id=device, device_id_type=MESH,
        )

    low, high = pl.ds(0, dl // 2), pl.ds(dl // 2, dl // 2)
    ways = (right_id, left_id)

    def own_part(p, kind):
        cols = ((low, high), (high, low))[kind]
        return [
            ag(6 * p + 2 * kind + side, tok_ref.at[pieces[p], cols[side]], tok.at[ch, pieces[p], cols[side]], ways[side])
            for side in range(2)
        ]

    def from_neighbour(p, kind, side):
        part = tok.at[(left, right)[side], pieces[p], ((low, high), (high, low))[kind][side]]
        return ag(6 * p + 2 * kind + side, part, part, ways[side])

    def from_far(p, side):
        part = tok.at[far, pieces[p], (low, high)[side]]
        return ag(6 * p + 4 + side, part, part, ways[side])

    own = [own_part(p, kind) for kind in range(2) for p in range(len(pieces))]
    onward = []
    for c in sum(own, []):
        c.start()

    def pass_on(p):
        for side in range(2):
            from_neighbour(p, 0, side).wait_recv()
            part = tok.at[(left, right)[side], pieces[p], (low, high)[side]]
            c = ag(6 * p + 4 + side, part, part, ways[side])
            c.start()
            onward.append([c])

    def rest(p):
        for side in range(2):
            from_neighbour(p, 1, side).wait_recv()

    def multiply(p, i, src, cols):
        part = dot(tok[src, spans[p], :], wall[pl.ds(pl.multiple_of(src * dl, dl), dl), cols])
        if i == 0:
            acc[spans[p], cols] = part
        else:
            acc[spans[p], cols] += part

    both = pl.ds(0, 2 * cl)

    rounds = [[along_z(1), along_z(-1)]]
    if zs > 4:
        rounds.append([along_z(2), along_z(-2)])
    if group > 1:
        rounds.append([in_group(k) for k in range(1, group)])

    def meet(r):
        for device in rounds[r]:
            pl.semaphore_signal(met.at[r], inc=1, device_id=device, device_id_type=MESH)

    def met_all(r):
        pl.semaphore_wait(met.at[r], len(rounds[r]))

    meet(0)
    locals_[0].wait()
    for h in range(2):
        turned = filt[pl.ds(h * half, half), :].T.reshape(n, cpd, half)
        wide[:, pl.ds(h * cpd, cpd), :] = turned
    fsend[...] = wide[...].astype(BF16)
    met_all(0)
    for r in range(1, len(rounds)):
        meet(r)
        if r == 1:
            locals_[1].wait()
            for c in weights[0]:
                c.wait()
            multiply(0, 0, ch, both)
        met_all(r)
    if len(rounds) < 2:
        locals_[1].wait()
        for c in weights[0]:
            c.wait()
        multiply(0, 0, ch, both)

    def scatter(src, dst, sem):
        def one(k, _):
            j, r = lax.rem(k, zs), group - 1 - k // zs
            odd = lax.rem(j, 2)
            dz = zs // 2 + (j // 2) * (1 - odd) - ((j + 1) // 2) * odd
            x = lax.rem(mate // 2 + r // 2, max(group // 2, 1))
            to = lax.rem(z + dz, zs) * group + x * 2 + lax.rem(mate + r, min(group, 2))
            pltpu.make_async_remote_copy(
                src_ref=src.at[to], dst_ref=dst.at[seq], send_sem=sem.at[0], recv_sem=sem.at[1],
                device_id=(to, ch), device_id_type=MESH,
            ).start()
            return 0

        lax.fori_loop(0, n - 1, one, 0)

    def await_all(ref, sem):
        part = ref.at[pl.ds(0, n - 1)]
        pltpu.make_async_copy(part, part, sem).wait()

    scatter(fsend, frecv, f_sem)
    frecv[seq] = fsend[seq]
    multiply(1, 0, ch, both)

    for p in range(len(pieces)):
        pass_on(p)
    rest(0)
    for w in weights[1:3]:
        for c in w:
            c.wait()
    multiply(0, 1, left, both)
    multiply(0, 2, right, both)
    for c in locals_[2:]:
        c.wait()

    tc, ts = twist[0], twist[1]

    def spectrum(load, spec):
        for pair in range(cpd // 2):
            c0, c1 = 2 * pair, 2 * pair + 1
            x = jnp.concatenate([load(c0), load(c1)], axis=1).astype(BF16)
            a = dot(first[...], x)
            for j, c in enumerate((c0, c1)):
                ar = a[:count, j * half:(j + 1) * half]
                ai = a[count:, j * half:(j + 1) * half]
                mid[pl.ds(c * count, count), pl.ds(0, half)] = (ar * tc + ai * ts).astype(BF16)
                mid[pl.ds(c * count, count), pl.ds(half, half)] = (ai * tc - ar * ts).astype(BF16)
        spec[...] = dot(mid[...], second[...])

    def restore(pr, pi, send):
        mid[:, pl.ds(0, half)] = pr.astype(BF16)
        mid[:, pl.ds(half, half)] = pi.astype(BF16)
        spec_g[...] = dot(mid[...], third[...])
        for pair in range(cpd // 2):
            two = []
            for c in (2 * pair, 2 * pair + 1):
                zr = spec_g[pl.ds(c * count, count), pl.ds(0, half)]
                zi = spec_g[pl.ds(c * count, count), pl.ds(half, half)]
                two.append(jnp.concatenate([zr * tc - zi * ts, zi * tc + zr * ts], axis=0).astype(BF16))
            y = dot(last[...], jnp.concatenate(two, axis=1))
            for j in range(2):
                for h in range(2):
                    fwide[pl.ds(h * cpd + 2 * pair + j, n, stride=2 * cpd), :] = (
                        y[h * n:(h + 1) * n, j * half:(j + 1) * half])
        send[...] = fwide[...].astype(BF16).reshape(n, 2 * cpd, half)

    def rows_of(low_ref, low_at, low_stride, high_ref, high_at, high_stride):
        return lambda c: jnp.concatenate(
            [low_ref[pl.ds(low_at + c, n, stride=low_stride), :],
             high_ref[pl.ds(high_at + c, n, stride=high_stride), :]], axis=0)


    def short(h, taps, col):
        cols = pl.ds(col, cl)
        return (
            taps[0:1, :] * proj[pl.ds(HALO + h * half, half), cols]
            + taps[1:2, :] * proj[pl.ds(HALO - 1 + h * half, half), cols]
            + taps[2:3, :] * proj[pl.ds(HALO - 2 + h * half, half), cols]
        )

    def finish(p, cols):
        proj[pl.ds(spans[p].start + HALO, spans[p].size), cols] = acc[spans[p], cols].astype(BF16).astype(F32)

    def gated(h, v):
        at = pl.ds(h * half, half)
        g = short(h, taps_g, cl)
        gate[at, :] = g
        base[at, :] = g * skip[...] * v
        return gout[at, :].astype(F32) * g

    for side in range(2):
        from_far(0, side).wait_recv()
    for c in weights[3]:
        c.wait()
    multiply(0, 3, far, both)
    finish(0, both)
    tail[...] = proj[pl.ds(rows, HALO), :].astype(BF16)
    tail_copy = pltpu.make_async_remote_copy(
        src_ref=tail, dst_ref=tail_in, send_sem=tail_sem.at[0], recv_sem=tail_sem.at[1],
        device_id=(lax.rem(seq + 1, n), ch), device_id_type=MESH,
    )
    tail_copy.start()
    v = short(1, taps_v, 0)
    vsend[1] = v.T.reshape(n, cpd, half).astype(BF16)
    scatter(vsend.at[1], vrecv.at[1], v_sem.at[1])
    vrecv[1, seq] = vsend[1, seq]
    wide[:, pl.ds(cpd, cpd), :] = gated(1, v).T.reshape(n, cpd, half)

    await_all(frecv, f_sem.at[1])
    fwide[...] = frecv[...].astype(F32).reshape(n * 2 * cpd, half)
    spectrum(rows_of(fwide, 0, 2 * cpd, fwide, cpd, 2 * cpd), spec_h)

    rest(1)
    multiply(1, 1, left, both)
    multiply(1, 2, right, both)
    tail_copy.wait_recv()
    proj[pl.ds(0, HALO), :] = jnp.where(seq > 0, tail_in[...].astype(F32), 0.0)
    value_cols, gate_cols = pl.ds(0, cl), pl.ds(cl, cl)
    for p in range(1, len(pieces)):
        for side in range(2):
            from_far(p, side).wait_recv()
    multiply(1, 3, far, value_cols)
    finish(1, value_cols)
    v = short(0, taps_v, 0)
    vsend[0] = v.T.reshape(n, cpd, half).astype(BF16)
    scatter(vsend.at[0], vrecv.at[0], v_sem.at[0])
    vrecv[0, seq] = vsend[0, seq]
    multiply(1, 3, far, gate_cols)
    finish(1, gate_cols)
    wide[:, pl.ds(0, cpd), :] = gated(0, v).T.reshape(n, cpd, half)
    msend[...] = wide[...].astype(BF16)
    scatter(msend, mrecv, m_sem)
    mrecv[seq] = msend[seq]

    for h in (1, 0):
        await_all(vrecv.at[h], v_sem.at[h, 1])
        vwide[h] = vrecv[h].astype(F32).reshape(n * cpd, half)
    spectrum(rows_of(vwide.at[0], 0, cpd, vwide.at[1], 0, cpd), spec_v)
    re, im = pl.ds(0, half), pl.ds(half, half)
    vr, vi = spec_v[:, re], spec_v[:, im]
    hr, hi = spec_h[:, re], spec_h[:, im]
    restore(vr * hr - vi * hi, vr * hi + vi * hr, csend)
    scatter(csend, crecv, c_sem)
    crecv[seq] = csend[seq]

    await_all(mrecv, m_sem.at[1])
    fwide[...] = mrecv[...].astype(F32).reshape(n * 2 * cpd, half)
    spectrum(rows_of(fwide, 0, 2 * cpd, fwide, cpd, 2 * cpd), spec_g)
    gr, gi = spec_g[:, re], spec_g[:, im]
    vr, vi = spec_v[:, re], spec_v[:, im]
    restore(gr * vr + gi * vi, gi * vr - gr * vi, gsend)
    scatter(gsend, grecv, g_sem)
    stays = pltpu.make_async_copy(gsend.at[seq], grecv.at[seq], own_sem.at[0])
    stays.start()

    await_all(crecv, c_sem.at[1])
    wide[...] = crecv[...].astype(F32)
    for h in range(2):
        at = pl.ds(h * half, half)
        y = wide[:, pl.ds(h * cpd, cpd), :].reshape(cl, half).T
        out[at, :] = (gate[at, :] * y + base[at, :]).astype(BF16)
    result = pltpu.make_async_copy(out, out_ref, own_sem.at[1])
    result.start()

    for c in sum(own + onward, [tail_copy]):
        c.wait_send()
    stays.wait()
    result.wait()
    await_all(fsend, f_sem.at[0])
    await_all(msend, m_sem.at[0])
    for h in range(2):
        await_all(vsend.at[h], v_sem.at[h, 0])
    await_all(csend, c_sem.at[0])
    await_all(grecv, g_sem.at[1])
    await_all(gsend, g_sem.at[0])


def closing_kernel(steps, grad_ref, out_in_ref, out_ref, fgrad_ref, grad, fgrad, sem):
    cpd = grad_ref.shape[1] // 2
    half = grad_ref.shape[2]
    blocks = grad_ref.shape[0] // steps
    columns = fgrad_ref.shape[1] // steps
    moved = pltpu.make_async_copy(out_in_ref, out_ref, sem.at[0])
    arrive, leave = [], []
    for i in range(steps):
        at, cols = pl.ds(i * blocks, blocks), pl.ds(i * columns, columns)
        arrive.append(pltpu.make_async_copy(grad_ref.at[at], grad.at[at], sem.at[1 + 2 * i]))
        leave.append(pltpu.make_async_copy(fgrad.at[:, cols], fgrad_ref.at[:, cols], sem.at[2 + 2 * i]))
    for c in arrive:
        c.start()
    moved.start()
    for i in range(steps):
        arrive[i].wait()
        x = grad[pl.ds(i * blocks, blocks)].astype(F32)
        for h in range(2):
            fgrad[pl.ds(h * half, half), pl.ds(i * columns, columns)] = (
                x[:, h * cpd:(h + 1) * cpd, :].reshape(columns, half).T)
        leave[i].start()
    for c in leave + [moved]:
        c.wait()


def shards(n, yn, tokens, w_value, w_gate, short_value, short_gate, skip_bias, long_filter, grad_out):
    rows, dl = tokens.shape
    d, cl = w_value.shape
    half = rows // 2
    cpd = cl // n
    count = 2 * n
    consts = tables(n, half)
    block = (n, 2 * cpd, half)
    small = (n, cpd, half)
    anywhere = pl.BlockSpec(memory_space=pl.ANY)
    dma = pltpu.SemaphoreType.DMA
    scratch = [
        pltpu.VMEM((yn, rows, dl), BF16),
        pltpu.VMEM((d, 2 * cl), BF16),
        pltpu.VMEM((3, cl), F32),
        pltpu.VMEM((3, cl), F32),
        pltpu.VMEM((1, cl), F32),
        pltpu.VMEM((rows, cl), F32),
        pltpu.VMEM((rows, cl), BF16),
        *[pltpu.VMEM(c.shape, c.dtype) for c in consts],
        pltpu.VMEM((rows, 2 * cl), F32),
        pltpu.VMEM((HALO + rows, 2 * cl), F32),
        pltpu.VMEM((HALO, 2 * cl), BF16),
        pltpu.VMEM((HALO, 2 * cl), BF16),
        pltpu.VMEM((rows, cl), F32),
        pltpu.VMEM((rows, cl), F32),
        pltpu.VMEM(block, BF16),
        pltpu.VMEM(block, BF16),
        pltpu.VMEM((2, *small), BF16),
        pltpu.VMEM((2, *small), BF16),
        pltpu.VMEM(block, BF16),
        pltpu.VMEM(block, BF16),
        pltpu.VMEM(block, BF16),
        pltpu.VMEM(block, BF16),
        pltpu.VMEM(block, BF16),
        pltpu.VMEM((rows, cl), BF16),
        pltpu.VMEM(block, F32),
        pltpu.VMEM((n * 2 * cpd, half), F32),
        pltpu.VMEM((2, n * cpd, half), F32),
        pltpu.VMEM((cpd * count, 2 * half), BF16),
        pltpu.VMEM((cpd * count, 2 * half), F32),
        pltpu.VMEM((cpd * count, 2 * half), F32),
        pltpu.VMEM((cpd * count, 2 * half), F32),
        dma((11,)),
        dma((2 * yn,)),
        dma((12,)),
        dma((12,)),
        dma((2,)),
        dma((2,)),
        dma((2,)),
        dma((2, 2)),
        dma((2,)),
        dma((2,)),
        dma((2,)),
        pltpu.SemaphoreType.REGULAR((3,)),
    ]
    grad, out = pl.pallas_call(
        functools.partial(transform_kernel, n, yn),
        out_shape=(
            jax.ShapeDtypeStruct(block, BF16),
            jax.ShapeDtypeStruct((rows, cl), BF16),
        ),
        in_specs=[anywhere] * 13,
        out_specs=[anywhere] * 2,
        scratch_shapes=scratch,
        compiler_params=pltpu.CompilerParams(
            collective_id=0, has_side_effects=True, vmem_limit_bytes=56 * 1024 * 1024
        ),
    )(tokens, w_value, w_gate, short_value, short_gate, skip_bias[None], long_filter, grad_out, *consts)
    steps = 4 if cl % 512 == 0 else 1
    return pl.pallas_call(
        functools.partial(closing_kernel, steps),
        out_shape=(
            jax.ShapeDtypeStruct((rows, cl), BF16),
            jax.ShapeDtypeStruct((rows, cl), F32),
        ),
        in_specs=[anywhere] * 2,
        out_specs=[anywhere] * 2,
        scratch_shapes=[pltpu.VMEM(block, BF16), pltpu.VMEM((rows, cl), F32), dma((1 + 2 * steps,))],
    )(grad, out)


def solution(mesh):
    return jax.shard_map(
        functools.partial(shards, mesh.shape["seq"], mesh.shape["ch"]),
        mesh=mesh,
        in_specs=(
            P("seq", "ch"),
            P(None, "ch"),
            P(None, "ch"),
            P(None, "ch"),
            P(None, "ch"),
            P("ch"),
            P("seq", "ch"),
            P("seq", "ch"),
        ),
        out_specs=(P("seq", "ch"), P("seq", "ch")),
        check_vma=False,
    )
```

```python
import functools
import math

import jax
import jax.numpy as jnp
import numpy as np
from jax import lax
from jax.experimental import pallas as pl
from jax.experimental.pallas import tpu as pltpu
from jax.sharding import PartitionSpec as P

MESH = pl.DeviceIdType.MESH
F32 = jnp.float32
BF16 = jnp.bfloat16
HALO = 16


def tables(blocks, half):
    count = 2 * blocks
    row = np.arange(count)
    q = 2 * (row % blocks) + row // blocks
    k = np.arange(count)
    angle = 2 * np.pi * ((k[:, None] * q[None, :]) % count + q[None, :] / 4) / count
    first = np.concatenate([np.cos(angle), -np.sin(angle)], axis=0)
    last = np.concatenate([np.cos(angle).T, -np.sin(angle).T], axis=1) / (count * half)
    l = np.arange(half)
    twist = 2 * np.pi * (k[:, None] + 0.25) * l[None, :] / (count * half)
    turn = 2 * np.pi * ((l[:, None] * l[None, :]) % half) / half
    c, s = np.cos(turn), np.sin(turn)
    second = np.block([[c, -s], [s, c]])
    third = np.block([[c, s], [-s, c]])
    return (
        jnp.asarray(first, BF16),
        jnp.asarray(second, BF16),
        jnp.asarray(third, BF16),
        jnp.asarray(last, BF16),
        jnp.asarray(np.stack([np.cos(twist), np.sin(twist)]), F32),
    )


def dot(a, b):
    return jnp.dot(a, b, preferred_element_type=F32)


def transform_kernel(
    n, yn,
    tok_ref, wv_ref, wg_ref, taps_v_ref, taps_g_ref, skip_ref, filt_ref, gout_ref,
    first_ref, second_ref, third_ref, last_ref, twist_ref,
    grecv, out_ref,
    tok, wall, taps_v, taps_g, skip, filt, gout, first, second, third, last, twist,
    acc, proj, tail, tail_in, gate, base,
    fsend, frecv, vsend, vrecv, msend, mrecv, csend, crecv, gsend, out,
    wide, fwide, vwide, mid, spec_v, spec_h, spec_g,
    loc_sem, w_sem, ag_send, ag_recv, tail_sem, own_sem,
    f_sem, v_sem, m_sem, c_sem, g_sem, met,
):
    seq = lax.axis_index("seq")
    ch = lax.axis_index("ch")
    rows, dl = tok_ref.shape
    cl = wv_ref.shape[1]
    half = rows // 2
    cpd = cl // n
    count = 2 * n
    group = 8 if n >= 32 else 1
    zs = n // group
    right, left = lax.rem(ch + 1, yn), lax.rem(ch + yn - 1, yn)
    far = lax.rem(ch + 2, yn)
    right_id, left_id = (seq, right), (seq, left)
    z, mate = seq // group, lax.rem(seq, group)

    def along_z(k):
        return (lax.rem(z + k + zs, zs) * group + mate, ch)

    def in_group(k):
        return (z * group + lax.rem(mate + k, group), ch)

    def local(i, src, dst):
        return pltpu.make_async_copy(src, dst, loc_sem.at[i])

    locals_ = [
        local(0, filt_ref, filt),
        local(1, tok_ref, tok.at[ch]),
        local(2, first_ref, first),
        local(3, second_ref, second),
        local(4, third_ref, third),
        local(5, last_ref, last),
        local(6, twist_ref, twist),
        local(7, taps_v_ref, taps_v),
        local(8, taps_g_ref, taps_g),
        local(9, skip_ref, skip),
        local(10, gout_ref, gout),
    ]

    def weight_copies(i, src):
        at = pl.ds(pl.multiple_of(src * dl, dl), dl)
        return [
            pltpu.make_async_copy(wv_ref.at[at], wall.at[at, pl.ds(0, cl)], w_sem.at[2 * i]),
            pltpu.make_async_copy(wg_ref.at[at], wall.at[at, pl.ds(cl, cl)], w_sem.at[2 * i + 1]),
        ]

    weights = [weight_copies(i, s) for i, s in enumerate((ch, left, right, far))]

    barrier = pltpu.get_barrier_semaphore()
    near = [right_id, left_id, along_z(1), along_z(-1)] + [in_group(k) for k in range(1, group)]
    for device in near:
        pl.semaphore_signal(barrier, inc=1, device_id=device, device_id_type=MESH)
    for c in locals_:
        c.start()
    for w in weights:
        for c in w:
            c.start()
    pl.semaphore_wait(barrier, len(near))

    cut = half - HALO
    spans = (pl.ds(cut, rows - cut), pl.ds(0, cut))
    pieces = spans

    def ag(i, src, dst, device):
        return pltpu.make_async_remote_copy(
            src_ref=src, dst_ref=dst, send_sem=ag_send.at[i], recv_sem=ag_recv.at[i],
            device_id=device, device_id_type=MESH,
        )

    low, high = pl.ds(0, dl // 2), pl.ds(dl // 2, dl // 2)
    ways = (right_id, left_id)

    def own_part(p, kind):
        cols = ((low, high), (high, low))[kind]
        return [
            ag(6 * p + 2 * kind + side, tok_ref.at[pieces[p], cols[side]], tok.at[ch, pieces[p], cols[side]], ways[side])
            for side in range(2)
        ]

    def from_neighbour(p, kind, side):
        part = tok.at[(left, right)[side], pieces[p], ((low, high), (high, low))[kind][side]]
        return ag(6 * p + 2 * kind + side, part, part, ways[side])

    def from_far(p, side):
        part = tok.at[far, pieces[p], (low, high)[side]]
        return ag(6 * p + 4 + side, part, part, ways[side])

    own = [own_part(p, kind) for kind in range(2) for p in range(len(pieces))]
    onward = []
    for c in sum(own, []):
        c.start()

    def pass_on(p):
        for side in range(2):
            from_neighbour(p, 0, side).wait_recv()
            part = tok.at[(left, right)[side], pieces[p], (low, high)[side]]
            c = ag(6 * p + 4 + side, part, part, ways[side])
            c.start()
            onward.append([c])

    def rest(p):
        for side in range(2):
            from_neighbour(p, 1, side).wait_recv()

    def multiply(p, i, src, cols):
        part = dot(tok[src, spans[p], :], wall[pl.ds(pl.multiple_of(src * dl, dl), dl), cols])
        if i == 0:
            acc[spans[p], cols] = part
        else:
            acc[spans[p], cols] += part

    both = pl.ds(0, 2 * cl)

    rounds = [[along_z(1), along_z(-1)]]
    if zs > 4:
        rounds.append([along_z(2), along_z(-2)])
    if group > 1:
        rounds.append([in_group(k) for k in range(1, group)])

    def meet(r):
        for device in rounds[r]:
            pl.semaphore_signal(met.at[r], inc=1, device_id=device, device_id_type=MESH)

    def met_all(r):
        pl.semaphore_wait(met.at[r], len(rounds[r]))

    meet(0)
    locals_[0].wait()
    for h in range(2):
        turned = filt[pl.ds(h * half, half), :].T.reshape(n, cpd, half)
        wide[:, pl.ds(h * cpd, cpd), :] = turned
    fsend[...] = wide[...].astype(BF16)
    met_all(0)
    for r in range(1, len(rounds)):
        meet(r)
        if r == 1:
            locals_[1].wait()
            for c in weights[0]:
                c.wait()
            multiply(0, 0, ch, both)
        met_all(r)
    if len(rounds) < 2:
        locals_[1].wait()
        for c in weights[0]:
            c.wait()
        multiply(0, 0, ch, both)

    def scatter(src, dst, sem):
        def one(k, _):
            j, r = lax.rem(k, zs), group - 1 - k // zs
            odd = lax.rem(j, 2)
            dz = zs // 2 + (j // 2) * (1 - odd) - ((j + 1) // 2) * odd
            x = lax.rem(mate // 2 + r // 2, max(group // 2, 1))
            to = lax.rem(z + dz, zs) * group + x * 2 + lax.rem(mate + r, min(group, 2))
            pltpu.make_async_remote_copy(
                src_ref=src.at[to], dst_ref=dst.at[seq], send_sem=sem.at[0], recv_sem=sem.at[1],
                device_id=(to, ch), device_id_type=MESH,
            ).start()
            return 0

        lax.fori_loop(0, n - 1, one, 0)

    def await_all(ref, sem):
        part = ref.at[pl.ds(0, n - 1)]
        pltpu.make_async_copy(part, part, sem).wait()

    scatter(fsend, frecv, f_sem)
    frecv[seq] = fsend[seq]
    multiply(1, 0, ch, both)

    for p in range(len(pieces)):
        pass_on(p)
    rest(0)
    for w in weights[1:3]:
        for c in w:
            c.wait()
    multiply(0, 1, left, both)
    multiply(0, 2, right, both)
    for c in locals_[2:]:
        c.wait()

    tc, ts = twist[0], twist[1]

    def spectrum(load, spec):
        for pair in range(cpd // 2):
            c0, c1 = 2 * pair, 2 * pair + 1
            x = jnp.concatenate([load(c0), load(c1)], axis=1).astype(BF16)
            a = dot(first[...], x)
            for j, c in enumerate((c0, c1)):
                ar = a[:count, j * half:(j + 1) * half]
                ai = a[count:, j * half:(j + 1) * half]
                mid[pl.ds(c * count, count), pl.ds(0, half)] = (ar * tc + ai * ts).astype(BF16)
                mid[pl.ds(c * count, count), pl.ds(half, half)] = (ai * tc - ar * ts).astype(BF16)
        spec[...] = dot(mid[...], second[...])

    def restore(pr, pi, send):
        mid[:, pl.ds(0, half)] = pr.astype(BF16)
        mid[:, pl.ds(half, half)] = pi.astype(BF16)
        spec_g[...] = dot(mid[...], third[...])
        for pair in range(cpd // 2):
            two = []
            for c in (2 * pair, 2 * pair + 1):
                zr = spec_g[pl.ds(c * count, count), pl.ds(0, half)]
                zi = spec_g[pl.ds(c * count, count), pl.ds(half, half)]
                two.append(jnp.concatenate([zr * tc - zi * ts, zi * tc + zr * ts], axis=0).astype(BF16))
            y = dot(last[...], jnp.concatenate(two, axis=1))
            for j in range(2):
                for h in range(2):
                    fwide[pl.ds(h * cpd + 2 * pair + j, n, stride=2 * cpd), :] = (
                        y[h * n:(h + 1) * n, j * half:(j + 1) * half])
        send[...] = fwide[...].astype(BF16).reshape(n, 2 * cpd, half)

    def rows_of(low_ref, low_at, low_stride, high_ref, high_at, high_stride):
        return lambda c: jnp.concatenate(
            [low_ref[pl.ds(low_at + c, n, stride=low_stride), :],
             high_ref[pl.ds(high_at + c, n, stride=high_stride), :]], axis=0)


    def short(h, taps, col):
        cols = pl.ds(col, cl)
        return (
            taps[0:1, :] * proj[pl.ds(HALO + h * half, half), cols]
            + taps[1:2, :] * proj[pl.ds(HALO - 1 + h * half, half), cols]
            + taps[2:3, :] * proj[pl.ds(HALO - 2 + h * half, half), cols]
        )

    def finish(p, cols):
        proj[pl.ds(spans[p].start + HALO, spans[p].size), cols] = acc[spans[p], cols].astype(BF16).astype(F32)

    def gated(h, v):
        at = pl.ds(h * half, half)
        g = short(h, taps_g, cl)
        gate[at, :] = g
        base[at, :] = g * skip[...] * v
        return gout[at, :].astype(F32) * g

    for side in range(2):
        from_far(0, side).wait_recv()
    for c in weights[3]:
        c.wait()
    multiply(0, 3, far, both)
    finish(0, both)
    tail[...] = proj[pl.ds(rows, HALO), :].astype(BF16)
    tail_copy = pltpu.make_async_remote_copy(
        src_ref=tail, dst_ref=tail_in, send_sem=tail_sem.at[0], recv_sem=tail_sem.at[1],
        device_id=(lax.rem(seq + 1, n), ch), device_id_type=MESH,
    )
    tail_copy.start()
    v = short(1, taps_v, 0)
    vsend[1] = v.T.reshape(n, cpd, half).astype(BF16)
    scatter(vsend.at[1], vrecv.at[1], v_sem.at[1])
    vrecv[1, seq] = vsend[1, seq]
    wide[:, pl.ds(cpd, cpd), :] = gated(1, v).T.reshape(n, cpd, half)

    rest(1)
    multiply(1, 1, left, both)
    multiply(1, 2, right, both)
    tail_copy.wait_recv()
    proj[pl.ds(0, HALO), :] = jnp.where(seq > 0, tail_in[...].astype(F32), 0.0)
    value_cols, gate_cols = pl.ds(0, cl), pl.ds(cl, cl)
    for p in range(1, len(pieces)):
        for side in range(2):
            from_far(p, side).wait_recv()
    multiply(1, 3, far, value_cols)
    finish(1, value_cols)
    v = short(0, taps_v, 0)
    vsend[0] = v.T.reshape(n, cpd, half).astype(BF16)
    scatter(vsend.at[0], vrecv.at[0], v_sem.at[0])
    vrecv[0, seq] = vsend[0, seq]
    multiply(1, 3, far, gate_cols)
    finish(1, gate_cols)
    wide[:, pl.ds(0, cpd), :] = gated(0, v).T.reshape(n, cpd, half)
    msend[...] = wide[...].astype(BF16)
    await_all(frecv, f_sem.at[1])
    fwide[...] = frecv[...].astype(F32).reshape(n * 2 * cpd, half)
    spectrum(rows_of(fwide, 0, 2 * cpd, fwide, cpd, 2 * cpd), spec_h)
    scatter(msend, mrecv, m_sem)
    mrecv[seq] = msend[seq]

    for h in (1, 0):
        await_all(vrecv.at[h], v_sem.at[h, 1])
        vwide[h] = vrecv[h].astype(F32).reshape(n * cpd, half)
    spectrum(rows_of(vwide.at[0], 0, cpd, vwide.at[1], 0, cpd), spec_v)
    re, im = pl.ds(0, half), pl.ds(half, half)
    vr, vi = spec_v[:, re], spec_v[:, im]
    hr, hi = spec_h[:, re], spec_h[:, im]
    restore(vr * hr - vi * hi, vr * hi + vi * hr, csend)
    scatter(csend, crecv, c_sem)
    crecv[seq] = csend[seq]

    await_all(mrecv, m_sem.at[1])
    fwide[...] = mrecv[...].astype(F32).reshape(n * 2 * cpd, half)
    spectrum(rows_of(fwide, 0, 2 * cpd, fwide, cpd, 2 * cpd), spec_g)
    gr, gi = spec_g[:, re], spec_g[:, im]
    vr, vi = spec_v[:, re], spec_v[:, im]
    restore(gr * vr + gi * vi, gi * vr - gr * vi, gsend)
    scatter(gsend, grecv, g_sem)
    stays = pltpu.make_async_copy(gsend.at[seq], grecv.at[seq], own_sem.at[0])
    stays.start()

    await_all(crecv, c_sem.at[1])
    wide[...] = crecv[...].astype(F32)
    for h in range(2):
        at = pl.ds(h * half, half)
        y = wide[:, pl.ds(h * cpd, cpd), :].reshape(cl, half).T
        out[at, :] = (gate[at, :] * y + base[at, :]).astype(BF16)
    result = pltpu.make_async_copy(out, out_ref, own_sem.at[1])
    result.start()

    for c in sum(own + onward, [tail_copy]):
        c.wait_send()
    stays.wait()
    result.wait()
    await_all(fsend, f_sem.at[0])
    await_all(msend, m_sem.at[0])
    for h in range(2):
        await_all(vsend.at[h], v_sem.at[h, 0])
    await_all(csend, c_sem.at[0])
    await_all(grecv, g_sem.at[1])
    await_all(gsend, g_sem.at[0])


def closing_kernel(grad_ref, out_in_ref, out_ref, fgrad_ref):
    cpd = grad_ref.shape[1] // 2
    half = grad_ref.shape[2]
    columns = out_ref.shape[1]
    out_ref[...] = out_in_ref[...]
    x = grad_ref[...].astype(F32)
    for h in range(2):
        fgrad_ref[pl.ds(h * half, half), :] = x[:, h * cpd:(h + 1) * cpd, :].reshape(columns, half).T


def shards(n, yn, tokens, w_value, w_gate, short_value, short_gate, skip_bias, long_filter, grad_out):
    rows, dl = tokens.shape
    d, cl = w_value.shape
    half = rows // 2
    cpd = cl // n
    count = 2 * n
    consts = tables(n, half)
    block = (n, 2 * cpd, half)
    small = (n, cpd, half)
    anywhere = pl.BlockSpec(memory_space=pl.ANY)
    dma = pltpu.SemaphoreType.DMA
    scratch = [
        pltpu.VMEM((yn, rows, dl), BF16),
        pltpu.VMEM((d, 2 * cl), BF16),
        pltpu.VMEM((3, cl), F32),
        pltpu.VMEM((3, cl), F32),
        pltpu.VMEM((1, cl), F32),
        pltpu.VMEM((rows, cl), F32),
        pltpu.VMEM((rows, cl), BF16),
        *[pltpu.VMEM(c.shape, c.dtype) for c in consts],
        pltpu.VMEM((rows, 2 * cl), F32),
        pltpu.VMEM((HALO + rows, 2 * cl), F32),
        pltpu.VMEM((HALO, 2 * cl), BF16),
        pltpu.VMEM((HALO, 2 * cl), BF16),
        pltpu.VMEM((rows, cl), F32),
        pltpu.VMEM((rows, cl), F32),
        pltpu.VMEM(block, BF16),
        pltpu.VMEM(block, BF16),
        pltpu.VMEM((2, *small), BF16),
        pltpu.VMEM((2, *small), BF16),
        pltpu.VMEM(block, BF16),
        pltpu.VMEM(block, BF16),
        pltpu.VMEM(block, BF16),
        pltpu.VMEM(block, BF16),
        pltpu.VMEM(block, BF16),
        pltpu.VMEM((rows, cl), BF16),
        pltpu.VMEM(block, F32),
        pltpu.VMEM((n * 2 * cpd, half), F32),
        pltpu.VMEM((2, n * cpd, half), F32),
        pltpu.VMEM((cpd * count, 2 * half), BF16),
        pltpu.VMEM((cpd * count, 2 * half), F32),
        pltpu.VMEM((cpd * count, 2 * half), F32),
        pltpu.VMEM((cpd * count, 2 * half), F32),
        dma((11,)),
        dma((2 * yn,)),
        dma((12,)),
        dma((12,)),
        dma((2,)),
        dma((2,)),
        dma((2,)),
        dma((2, 2)),
        dma((2,)),
        dma((2,)),
        dma((2,)),
        pltpu.SemaphoreType.REGULAR((3,)),
    ]
    grad, out = pl.pallas_call(
        functools.partial(transform_kernel, n, yn),
        out_shape=(
            jax.ShapeDtypeStruct(block, BF16),
            jax.ShapeDtypeStruct((rows, cl), BF16),
        ),
        in_specs=[anywhere] * 13,
        out_specs=[anywhere] * 2,
        scratch_shapes=scratch,
        compiler_params=pltpu.CompilerParams(
            collective_id=0, has_side_effects=True, vmem_limit_bytes=56 * 1024 * 1024
        ),
    )(tokens, w_value, w_gate, short_value, short_gate, skip_bias[None], long_filter, grad_out, *consts)
    steps = 2
    blocks = pl.BlockSpec((n // steps, 2 * cpd, half), lambda i: (i, 0, 0))
    columns = pl.BlockSpec((rows, cl // steps), lambda i: (0, i))
    return pl.pallas_call(
        closing_kernel,
        grid=(steps,),
        out_shape=(
            jax.ShapeDtypeStruct((rows, cl), BF16),
            jax.ShapeDtypeStruct((rows, cl), F32),
        ),
        in_specs=[blocks, columns],
        out_specs=(columns, columns),
    )(grad, out)


def solution(mesh):
    return jax.shard_map(
        functools.partial(shards, mesh.shape["seq"], mesh.shape["ch"]),
        mesh=mesh,
        in_specs=(
            P("seq", "ch"),
            P(None, "ch"),
            P(None, "ch"),
            P(None, "ch"),
            P(None, "ch"),
            P("ch"),
            P("seq", "ch"),
            P("seq", "ch"),
        ),
        out_specs=(P("seq", "ch"), P("seq", "ch")),
        check_vma=False,
    )
```

```python
import functools
import math

import jax
import jax.numpy as jnp
import numpy as np
from jax import lax
from jax.experimental import pallas as pl
from jax.experimental.pallas import tpu as pltpu
from jax.sharding import PartitionSpec as P

MESH = pl.DeviceIdType.MESH
F32 = jnp.float32
BF16 = jnp.bfloat16
HALO = 16


def tables(blocks, half):
    count = 2 * blocks
    row = np.arange(count)
    q = 2 * (row % blocks) + row // blocks
    k = np.arange(count)
    angle = 2 * np.pi * ((k[:, None] * q[None, :]) % count + q[None, :] / 4) / count
    first = np.concatenate([np.cos(angle), -np.sin(angle)], axis=0)
    last = np.concatenate([np.cos(angle).T, -np.sin(angle).T], axis=1) / (count * half)
    l = np.arange(half)
    twist = 2 * np.pi * (k[:, None] + 0.25) * l[None, :] / (count * half)
    turn = 2 * np.pi * ((l[:, None] * l[None, :]) % half) / half
    c, s = np.cos(turn), np.sin(turn)
    second = np.block([[c, -s], [s, c]])
    third = np.block([[c, s], [-s, c]])
    return (
        jnp.asarray(first, BF16),
        jnp.asarray(second, BF16),
        jnp.asarray(third, BF16),
        jnp.asarray(last, BF16),
        jnp.asarray(np.stack([np.cos(twist), np.sin(twist)]), F32),
    )


def dot(a, b):
    return jnp.dot(a, b, preferred_element_type=F32)


def transform_kernel(
    n, yn,
    tok_ref, wv_ref, wg_ref, taps_v_ref, taps_g_ref, skip_ref, filt_ref, gout_ref,
    first_ref, second_ref, third_ref, last_ref, twist_ref,
    grecv, out_ref,
    tok, wall, taps_v, taps_g, skip, filt, gout, first, second, third, last, twist,
    acc, proj, tail, tail_in, gate, base,
    fsend, frecv, vsend, vrecv, msend, mrecv, csend, crecv, gsend, out,
    wide, fwide, vwide, mid, spec_v, spec_h, spec_g,
    loc_sem, w_sem, ag_send, ag_recv, tail_sem, own_sem,
    f_sem, v_sem, m_sem, c_sem, g_sem, met,
):
    seq = lax.axis_index("seq")
    ch = lax.axis_index("ch")
    rows, dl = tok_ref.shape
    cl = wv_ref.shape[1]
    half = rows // 2
    cpd = cl // n
    count = 2 * n
    group = 8 if n >= 32 else 1
    zs = n // group
    right, left = lax.rem(ch + 1, yn), lax.rem(ch + yn - 1, yn)
    far = lax.rem(ch + 2, yn)
    right_id, left_id = (seq, right), (seq, left)
    z, mate = seq // group, lax.rem(seq, group)

    def along_z(k):
        return (lax.rem(z + k + zs, zs) * group + mate, ch)

    def in_group(k):
        return (z * group + lax.rem(mate + k, group), ch)

    def local(i, src, dst):
        return pltpu.make_async_copy(src, dst, loc_sem.at[i])

    locals_ = [
        local(0, filt_ref, filt),
        local(1, tok_ref, tok.at[ch]),
        local(2, first_ref, first),
        local(3, second_ref, second),
        local(4, third_ref, third),
        local(5, last_ref, last),
        local(6, twist_ref, twist),
        local(7, taps_v_ref, taps_v),
        local(8, taps_g_ref, taps_g),
        local(9, skip_ref, skip),
        local(10, gout_ref, gout),
    ]

    def weight_copies(i, src):
        at = pl.ds(pl.multiple_of(src * dl, dl), dl)
        return [
            pltpu.make_async_copy(wv_ref.at[at], wall.at[at, pl.ds(0, cl)], w_sem.at[2 * i]),
            pltpu.make_async_copy(wg_ref.at[at], wall.at[at, pl.ds(cl, cl)], w_sem.at[2 * i + 1]),
        ]

    weights = [weight_copies(i, s) for i, s in enumerate((ch, left, right, far))]

    barrier = pltpu.get_barrier_semaphore()
    near = [right_id, left_id, along_z(1), along_z(-1)] + [in_group(k) for k in range(1, group)]
    for device in near:
        pl.semaphore_signal(barrier, inc=1, device_id=device, device_id_type=MESH)
    for c in locals_:
        c.start()
    for w in weights:
        for c in w:
            c.start()
    pl.semaphore_wait(barrier, len(near))

    cut = half - HALO
    spans = (pl.ds(cut, rows - cut), pl.ds(0, cut))
    pieces = spans

    def ag(i, src, dst, device):
        return pltpu.make_async_remote_copy(
            src_ref=src, dst_ref=dst, send_sem=ag_send.at[i], recv_sem=ag_recv.at[i],
            device_id=device, device_id_type=MESH,
        )

    low, high = pl.ds(0, dl // 2), pl.ds(dl // 2, dl // 2)
    ways = (right_id, left_id)

    def own_part(p, kind):
        cols = ((low, high), (high, low))[kind]
        return [
            ag(6 * p + 2 * kind + side, tok_ref.at[pieces[p], cols[side]], tok.at[ch, pieces[p], cols[side]], ways[side])
            for side in range(2)
        ]

    def from_neighbour(p, kind, side):
        part = tok.at[(left, right)[side], pieces[p], ((low, high), (high, low))[kind][side]]
        return ag(6 * p + 2 * kind + side, part, part, ways[side])

    def from_far(p, side):
        part = tok.at[far, pieces[p], (low, high)[side]]
        return ag(6 * p + 4 + side, part, part, ways[side])

    own = [own_part(0, 0), own_part(0, 1), own_part(1, 0)]
    delayed = own_part(1, 1)
    onward = []
    for c in sum(own, []):
        c.start()

    def pass_on(p):
        for side in range(2):
            from_neighbour(p, 0, side).wait_recv()
            part = tok.at[(left, right)[side], pieces[p], (low, high)[side]]
            c = ag(6 * p + 4 + side, part, part, ways[side])
            c.start()
            onward.append([c])

    def rest(p):
        for side in range(2):
            from_neighbour(p, 1, side).wait_recv()

    def multiply(p, i, src, cols):
        part = dot(tok[src, spans[p], :], wall[pl.ds(pl.multiple_of(src * dl, dl), dl), cols])
        if i == 0:
            acc[spans[p], cols] = part
        else:
            acc[spans[p], cols] += part

    both = pl.ds(0, 2 * cl)

    rounds = [[along_z(1), along_z(-1)]]
    if zs > 4:
        rounds.append([along_z(2), along_z(-2)])
    if group > 1:
        rounds.append([in_group(k) for k in range(1, group)])

    def meet(r):
        for device in rounds[r]:
            pl.semaphore_signal(met.at[r], inc=1, device_id=device, device_id_type=MESH)

    def met_all(r):
        pl.semaphore_wait(met.at[r], len(rounds[r]))

    meet(0)
    locals_[0].wait()
    for h in range(2):
        turned = filt[pl.ds(h * half, half), :].T.reshape(n, cpd, half)
        wide[:, pl.ds(h * cpd, cpd), :] = turned
    fsend[...] = wide[...].astype(BF16)
    met_all(0)
    for r in range(1, len(rounds)):
        meet(r)
        if r == 1:
            locals_[1].wait()
            for c in weights[0]:
                c.wait()
            multiply(0, 0, ch, both)
        met_all(r)
    if len(rounds) < 2:
        locals_[1].wait()
        for c in weights[0]:
            c.wait()
        multiply(0, 0, ch, both)

    def scatter(src, dst, sem):
        def one(k, _):
            j, r = lax.rem(k, zs), group - 1 - k // zs
            odd = lax.rem(j, 2)
            dz = zs // 2 + (j // 2) * (1 - odd) - ((j + 1) // 2) * odd
            x = lax.rem(mate // 2 + r // 2, max(group // 2, 1))
            to = lax.rem(z + dz, zs) * group + x * 2 + lax.rem(mate + r, min(group, 2))
            pltpu.make_async_remote_copy(
                src_ref=src.at[to], dst_ref=dst.at[seq], send_sem=sem.at[0], recv_sem=sem.at[1],
                device_id=(to, ch), device_id_type=MESH,
            ).start()
            return 0

        lax.fori_loop(0, n - 1, one, 0)

    def await_all(ref, sem):
        part = ref.at[pl.ds(0, n - 1)]
        pltpu.make_async_copy(part, part, sem).wait()

    scatter(fsend, frecv, f_sem)
    frecv[seq] = fsend[seq]
    multiply(1, 0, ch, both)

    pass_on(0)
    for c in delayed:
        c.start()
    own.append(delayed)
    pass_on(1)
    rest(0)
    for w in weights[1:3]:
        for c in w:
            c.wait()
    multiply(0, 1, left, both)
    multiply(0, 2, right, both)
    for c in locals_[2:]:
        c.wait()

    tc, ts = twist[0], twist[1]

    def spectrum(load, spec):
        for pair in range(cpd // 2):
            c0, c1 = 2 * pair, 2 * pair + 1
            x = jnp.concatenate([load(c0), load(c1)], axis=1).astype(BF16)
            a = dot(first[...], x)
            for j, c in enumerate((c0, c1)):
                ar = a[:count, j * half:(j + 1) * half]
                ai = a[count:, j * half:(j + 1) * half]
                mid[pl.ds(c * count, count), pl.ds(0, half)] = (ar * tc + ai * ts).astype(BF16)
                mid[pl.ds(c * count, count), pl.ds(half, half)] = (ai * tc - ar * ts).astype(BF16)
        spec[...] = dot(mid[...], second[...])

    def restore(pr, pi, send):
        mid[:, pl.ds(0, half)] = pr.astype(BF16)
        mid[:, pl.ds(half, half)] = pi.astype(BF16)
        spec_g[...] = dot(mid[...], third[...])
        for pair in range(cpd // 2):
            two = []
            for c in (2 * pair, 2 * pair + 1):
                zr = spec_g[pl.ds(c * count, count), pl.ds(0, half)]
                zi = spec_g[pl.ds(c * count, count), pl.ds(half, half)]
                two.append(jnp.concatenate([zr * tc - zi * ts, zi * tc + zr * ts], axis=0).astype(BF16))
            y = dot(last[...], jnp.concatenate(two, axis=1))
            for j in range(2):
                for h in range(2):
                    fwide[pl.ds(h * cpd + 2 * pair + j, n, stride=2 * cpd), :] = (
                        y[h * n:(h + 1) * n, j * half:(j + 1) * half])
        send[...] = fwide[...].astype(BF16).reshape(n, 2 * cpd, half)

    def rows_of(low_ref, low_at, low_stride, high_ref, high_at, high_stride):
        return lambda c: jnp.concatenate(
            [low_ref[pl.ds(low_at + c, n, stride=low_stride), :],
             high_ref[pl.ds(high_at + c, n, stride=high_stride), :]], axis=0)


    def short(h, taps, col):
        cols = pl.ds(col, cl)
        return (
            taps[0:1, :] * proj[pl.ds(HALO + h * half, half), cols]
            + taps[1:2, :] * proj[pl.ds(HALO - 1 + h * half, half), cols]
            + taps[2:3, :] * proj[pl.ds(HALO - 2 + h * half, half), cols]
        )

    def finish(p, cols):
        proj[pl.ds(spans[p].start + HALO, spans[p].size), cols] = acc[spans[p], cols].astype(BF16).astype(F32)

    def gated(h, v):
        at = pl.ds(h * half, half)
        g = short(h, taps_g, cl)
        gate[at, :] = g
        base[at, :] = g * skip[...] * v
        return gout[at, :].astype(F32) * g

    for side in range(2):
        from_far(0, side).wait_recv()
    for c in weights[3]:
        c.wait()
    multiply(0, 3, far, both)
    finish(0, both)
    tail[...] = proj[pl.ds(rows, HALO), :].astype(BF16)
    tail_copy = pltpu.make_async_remote_copy(
        src_ref=tail, dst_ref=tail_in, send_sem=tail_sem.at[0], recv_sem=tail_sem.at[1],
        device_id=(lax.rem(seq + 1, n), ch), device_id_type=MESH,
    )
    tail_copy.start()
    v = short(1, taps_v, 0)
    vsend[1] = v.T.reshape(n, cpd, half).astype(BF16)
    scatter(vsend.at[1], vrecv.at[1], v_sem.at[1])
    vrecv[1, seq] = vsend[1, seq]
    wide[:, pl.ds(cpd, cpd), :] = gated(1, v).T.reshape(n, cpd, half)

    rest(1)
    multiply(1, 1, left, both)
    multiply(1, 2, right, both)
    tail_copy.wait_recv()
    proj[pl.ds(0, HALO), :] = jnp.where(seq > 0, tail_in[...].astype(F32), 0.0)
    value_cols, gate_cols = pl.ds(0, cl), pl.ds(cl, cl)
    for p in range(1, len(pieces)):
        for side in range(2):
            from_far(p, side).wait_recv()
    multiply(1, 3, far, value_cols)
    finish(1, value_cols)
    v = short(0, taps_v, 0)
    vsend[0] = v.T.reshape(n, cpd, half).astype(BF16)
    scatter(vsend.at[0], vrecv.at[0], v_sem.at[0])
    vrecv[0, seq] = vsend[0, seq]
    multiply(1, 3, far, gate_cols)
    finish(1, gate_cols)
    wide[:, pl.ds(0, cpd), :] = gated(0, v).T.reshape(n, cpd, half)
    msend[...] = wide[...].astype(BF16)
    await_all(frecv, f_sem.at[1])
    fwide[...] = frecv[...].astype(F32).reshape(n * 2 * cpd, half)
    spectrum(rows_of(fwide, 0, 2 * cpd, fwide, cpd, 2 * cpd), spec_h)
    scatter(msend, mrecv, m_sem)
    mrecv[seq] = msend[seq]

    for h in (1, 0):
        await_all(vrecv.at[h], v_sem.at[h, 1])
        vwide[h] = vrecv[h].astype(F32).reshape(n * cpd, half)
    spectrum(rows_of(vwide.at[0], 0, cpd, vwide.at[1], 0, cpd), spec_v)
    re, im = pl.ds(0, half), pl.ds(half, half)
    vr, vi = spec_v[:, re], spec_v[:, im]
    hr, hi = spec_h[:, re], spec_h[:, im]
    restore(vr * hr - vi * hi, vr * hi + vi * hr, csend)
    scatter(csend, crecv, c_sem)
    crecv[seq] = csend[seq]

    await_all(mrecv, m_sem.at[1])
    fwide[...] = mrecv[...].astype(F32).reshape(n * 2 * cpd, half)
    spectrum(rows_of(fwide, 0, 2 * cpd, fwide, cpd, 2 * cpd), spec_g)
    gr, gi = spec_g[:, re], spec_g[:, im]
    vr, vi = spec_v[:, re], spec_v[:, im]
    restore(gr * vr + gi * vi, gi * vr - gr * vi, gsend)
    scatter(gsend, grecv, g_sem)
    stays = pltpu.make_async_copy(gsend.at[seq], grecv.at[seq], own_sem.at[0])
    stays.start()

    await_all(crecv, c_sem.at[1])
    wide[...] = crecv[...].astype(F32)
    for h in range(2):
        at = pl.ds(h * half, half)
        y = wide[:, pl.ds(h * cpd, cpd), :].reshape(cl, half).T
        out[at, :] = (gate[at, :] * y + base[at, :]).astype(BF16)
    result = pltpu.make_async_copy(out, out_ref, own_sem.at[1])
    result.start()

    for c in sum(own + onward, [tail_copy]):
        c.wait_send()
    stays.wait()
    result.wait()
    await_all(fsend, f_sem.at[0])
    await_all(msend, m_sem.at[0])
    for h in range(2):
        await_all(vsend.at[h], v_sem.at[h, 0])
    await_all(csend, c_sem.at[0])
    await_all(grecv, g_sem.at[1])
    await_all(gsend, g_sem.at[0])


def closing_kernel(grad_ref, out_in_ref, out_ref, fgrad_ref):
    cpd = grad_ref.shape[1] // 2
    half = grad_ref.shape[2]
    columns = out_ref.shape[1]
    out_ref[...] = out_in_ref[...]
    x = grad_ref[...].astype(F32)
    for h in range(2):
        fgrad_ref[pl.ds(h * half, half), :] = x[:, h * cpd:(h + 1) * cpd, :].reshape(columns, half).T


def shards(n, yn, tokens, w_value, w_gate, short_value, short_gate, skip_bias, long_filter, grad_out):
    rows, dl = tokens.shape
    d, cl = w_value.shape
    half = rows // 2
    cpd = cl // n
    count = 2 * n
    consts = tables(n, half)
    block = (n, 2 * cpd, half)
    small = (n, cpd, half)
    anywhere = pl.BlockSpec(memory_space=pl.ANY)
    dma = pltpu.SemaphoreType.DMA
    scratch = [
        pltpu.VMEM((yn, rows, dl), BF16),
        pltpu.VMEM((d, 2 * cl), BF16),
        pltpu.VMEM((3, cl), F32),
        pltpu.VMEM((3, cl), F32),
        pltpu.VMEM((1, cl), F32),
        pltpu.VMEM((rows, cl), F32),
        pltpu.VMEM((rows, cl), BF16),
        *[pltpu.VMEM(c.shape, c.dtype) for c in consts],
        pltpu.VMEM((rows, 2 * cl), F32),
        pltpu.VMEM((HALO + rows, 2 * cl), F32),
        pltpu.VMEM((HALO, 2 * cl), BF16),
        pltpu.VMEM((HALO, 2 * cl), BF16),
        pltpu.VMEM((rows, cl), F32),
        pltpu.VMEM((rows, cl), F32),
        pltpu.VMEM(block, BF16),
        pltpu.VMEM(block, BF16),
        pltpu.VMEM((2, *small), BF16),
        pltpu.VMEM((2, *small), BF16),
        pltpu.VMEM(block, BF16),
        pltpu.VMEM(block, BF16),
        pltpu.VMEM(block, BF16),
        pltpu.VMEM(block, BF16),
        pltpu.VMEM(block, BF16),
        pltpu.VMEM((rows, cl), BF16),
        pltpu.VMEM(block, F32),
        pltpu.VMEM((n * 2 * cpd, half), F32),
        pltpu.VMEM((2, n * cpd, half), F32),
        pltpu.VMEM((cpd * count, 2 * half), BF16),
        pltpu.VMEM((cpd * count, 2 * half), F32),
        pltpu.VMEM((cpd * count, 2 * half), F32),
        pltpu.VMEM((cpd * count, 2 * half), F32),
        dma((11,)),
        dma((2 * yn,)),
        dma((12,)),
        dma((12,)),
        dma((2,)),
        dma((2,)),
        dma((2,)),
        dma((2, 2)),
        dma((2,)),
        dma((2,)),
        dma((2,)),
        pltpu.SemaphoreType.REGULAR((3,)),
    ]
    grad, out = pl.pallas_call(
        functools.partial(transform_kernel, n, yn),
        out_shape=(
            jax.ShapeDtypeStruct(block, BF16),
            jax.ShapeDtypeStruct((rows, cl), BF16),
        ),
        in_specs=[anywhere] * 13,
        out_specs=[anywhere] * 2,
        scratch_shapes=scratch,
        compiler_params=pltpu.CompilerParams(
            collective_id=0, has_side_effects=True, vmem_limit_bytes=56 * 1024 * 1024
        ),
    )(tokens, w_value, w_gate, short_value, short_gate, skip_bias[None], long_filter, grad_out, *consts)
    steps = 2
    blocks = pl.BlockSpec((n // steps, 2 * cpd, half), lambda i: (i, 0, 0))
    columns = pl.BlockSpec((rows, cl // steps), lambda i: (0, i))
    return pl.pallas_call(
        closing_kernel,
        grid=(steps,),
        out_shape=(
            jax.ShapeDtypeStruct((rows, cl), BF16),
            jax.ShapeDtypeStruct((rows, cl), F32),
        ),
        in_specs=[blocks, columns],
        out_specs=(columns, columns),
    )(grad, out)


def solution(mesh):
    return jax.shard_map(
        functools.partial(shards, mesh.shape["seq"], mesh.shape["ch"]),
        mesh=mesh,
        in_specs=(
            P("seq", "ch"),
            P(None, "ch"),
            P(None, "ch"),
            P(None, "ch"),
            P(None, "ch"),
            P("ch"),
            P("seq", "ch"),
            P("seq", "ch"),
        ),
        out_specs=(P("seq", "ch"), P("seq", "ch")),
        check_vma=False,
    )
```

```python
import functools
import math

import jax
import jax.numpy as jnp
import numpy as np
from jax import lax
from jax.experimental import pallas as pl
from jax.experimental.pallas import tpu as pltpu
from jax.sharding import PartitionSpec as P

MESH = pl.DeviceIdType.MESH
F32 = jnp.float32
BF16 = jnp.bfloat16
HALO = 16


def tables(blocks, half):
    count = 2 * blocks
    row = np.arange(count)
    q = 2 * (row % blocks) + row // blocks
    k = np.arange(count)
    angle = 2 * np.pi * ((k[:, None] * q[None, :]) % count + q[None, :] / 4) / count
    first = np.concatenate([np.cos(angle), -np.sin(angle)], axis=0)
    last = np.concatenate([np.cos(angle).T, -np.sin(angle).T], axis=1) / (count * half)
    l = np.arange(half)
    twist = 2 * np.pi * (k[:, None] + 0.25) * l[None, :] / (count * half)
    turn = 2 * np.pi * ((l[:, None] * l[None, :]) % half) / half
    c, s = np.cos(turn), np.sin(turn)
    second = np.block([[c, -s], [s, c]])
    third = np.block([[c, s], [-s, c]])
    return (
        jnp.asarray(first, BF16),
        jnp.asarray(second, BF16),
        jnp.asarray(third, BF16),
        jnp.asarray(last, BF16),
        jnp.asarray(np.stack([np.cos(twist), np.sin(twist)]), F32),
    )


def dot(a, b):
    return jnp.dot(a, b, preferred_element_type=F32)


def transform_kernel(
    n, yn,
    tok_ref, wv_ref, wg_ref, taps_v_ref, taps_g_ref, skip_ref, filt_ref, gout_ref,
    first_ref, second_ref, third_ref, last_ref, twist_ref,
    grecv, out_ref,
    tok, wall, taps_v, taps_g, skip, filt, gout, first, second, third, last, twist,
    acc, proj, tail, tail_in, gate, base,
    fsend, frecv, vsend, vrecv, msend, mrecv, csend, crecv, gsend, out,
    wide, fwide, vwide, mid, spec_v, spec_h, spec_g,
    loc_sem, w_sem, ag_send, ag_recv, tail_sem, own_sem,
    f_sem, v_sem, m_sem, c_sem, g_sem, met,
):
    seq = lax.axis_index("seq")
    ch = lax.axis_index("ch")
    rows, dl = tok_ref.shape
    cl = wv_ref.shape[1]
    half = rows // 2
    cpd = cl // n
    count = 2 * n
    group = 8 if n >= 32 else 1
    zs = n // group
    right, left = lax.rem(ch + 1, yn), lax.rem(ch + yn - 1, yn)
    far = lax.rem(ch + 2, yn)
    right_id, left_id = (seq, right), (seq, left)
    z, mate = seq // group, lax.rem(seq, group)

    def along_z(k):
        return (lax.rem(z + k + zs, zs) * group + mate, ch)

    def in_group(k):
        return (z * group + lax.rem(mate + k, group), ch)

    def local(i, src, dst):
        return pltpu.make_async_copy(src, dst, loc_sem.at[i])

    locals_ = [
        local(0, filt_ref, filt),
        local(1, tok_ref, tok.at[ch]),
        local(2, first_ref, first),
        local(3, second_ref, second),
        local(4, third_ref, third),
        local(5, last_ref, last),
        local(6, twist_ref, twist),
        local(7, taps_v_ref, taps_v),
        local(8, taps_g_ref, taps_g),
        local(9, skip_ref, skip),
        local(10, gout_ref, gout),
    ]

    def weight_copies(i, src):
        at = pl.ds(pl.multiple_of(src * dl, dl), dl)
        return [
            pltpu.make_async_copy(wv_ref.at[at], wall.at[at, pl.ds(0, cl)], w_sem.at[2 * i]),
            pltpu.make_async_copy(wg_ref.at[at], wall.at[at, pl.ds(cl, cl)], w_sem.at[2 * i + 1]),
        ]

    weights = [weight_copies(i, s) for i, s in enumerate((ch, left, right, far))]

    barrier = pltpu.get_barrier_semaphore()
    near = [right_id, left_id, along_z(1), along_z(-1)] + [in_group(k) for k in range(1, group)]
    for device in near:
        pl.semaphore_signal(barrier, inc=1, device_id=device, device_id_type=MESH)
    for c in locals_:
        c.start()
    for w in weights:
        for c in w:
            c.start()
    pl.semaphore_wait(barrier, len(near))

    cut = half - HALO
    spans = (pl.ds(cut, rows - cut), pl.ds(0, cut))
    pieces = spans

    def ag(i, src, dst, device):
        return pltpu.make_async_remote_copy(
            src_ref=src, dst_ref=dst, send_sem=ag_send.at[i], recv_sem=ag_recv.at[i],
            device_id=device, device_id_type=MESH,
        )

    low, high = pl.ds(0, dl // 2), pl.ds(dl // 2, dl // 2)
    ways = (right_id, left_id)

    def own_part(p, kind):
        cols = ((low, high), (high, low))[kind]
        return [
            ag(6 * p + 2 * kind + side, tok_ref.at[pieces[p], cols[side]], tok.at[ch, pieces[p], cols[side]], ways[side])
            for side in range(2)
        ]

    def from_neighbour(p, kind, side):
        part = tok.at[(left, right)[side], pieces[p], ((low, high), (high, low))[kind][side]]
        return ag(6 * p + 2 * kind + side, part, part, ways[side])

    def from_far(p, side):
        part = tok.at[far, pieces[p], (low, high)[side]]
        return ag(6 * p + 4 + side, part, part, ways[side])

    own = [own_part(0, 0), own_part(0, 1), own_part(1, 0)]
    delayed = own_part(1, 1)
    onward = []
    for c in sum(own, []):
        c.start()

    def pass_on(p):
        for side in range(2):
            from_neighbour(p, 0, side).wait_recv()
            part = tok.at[(left, right)[side], pieces[p], (low, high)[side]]
            c = ag(6 * p + 4 + side, part, part, ways[side])
            c.start()
            onward.append([c])

    def rest(p):
        for side in range(2):
            from_neighbour(p, 1, side).wait_recv()

    def multiply(p, i, src, cols):
        part = dot(tok[src, spans[p], :], wall[pl.ds(pl.multiple_of(src * dl, dl), dl), cols])
        if i == 0:
            acc[spans[p], cols] = part
        else:
            acc[spans[p], cols] += part

    both = pl.ds(0, 2 * cl)

    rounds = [[along_z(1), along_z(-1)]]
    if zs > 4:
        rounds.append([along_z(2), along_z(-2)])
    if group > 1:
        rounds.append([in_group(k) for k in range(1, group)])

    def meet(r):
        for device in rounds[r]:
            pl.semaphore_signal(met.at[r], inc=1, device_id=device, device_id_type=MESH)

    def met_all(r):
        pl.semaphore_wait(met.at[r], len(rounds[r]))

    meet(0)
    locals_[0].wait()
    for h in range(2):
        turned = filt[pl.ds(h * half, half), :].T.reshape(n, cpd, half)
        wide[:, pl.ds(h * cpd, cpd), :] = turned
    fsend[...] = wide[...].astype(BF16)
    met_all(0)
    for r in range(1, len(rounds)):
        meet(r)
        if r == 1:
            locals_[1].wait()
            for c in weights[0]:
                c.wait()
            multiply(0, 0, ch, both)
        met_all(r)
    if len(rounds) < 2:
        locals_[1].wait()
        for c in weights[0]:
            c.wait()
        multiply(0, 0, ch, both)

    def scatter(src, dst, sem):
        def one(k, _):
            j, r = lax.rem(k, zs), group - 1 - k // zs
            odd = lax.rem(j, 2)
            dz = zs // 2 + (j // 2) * (1 - odd) - ((j + 1) // 2) * odd
            x = lax.rem(mate // 2 + r // 2, max(group // 2, 1))
            to = lax.rem(z + dz, zs) * group + x * 2 + lax.rem(mate + r, min(group, 2))
            pltpu.make_async_remote_copy(
                src_ref=src.at[to], dst_ref=dst.at[seq], send_sem=sem.at[0], recv_sem=sem.at[1],
                device_id=(to, ch), device_id_type=MESH,
            ).start()
            return 0

        lax.fori_loop(0, n - 1, one, 0)

    def await_all(ref, sem):
        part = ref.at[pl.ds(0, n - 1)]
        pltpu.make_async_copy(part, part, sem).wait()

    scatter(fsend, frecv, f_sem)
    frecv[seq] = fsend[seq]
    multiply(1, 0, ch, both)

    pass_on(0)
    pass_on(1)
    for c in delayed:
        c.start()
    own.append(delayed)
    rest(0)
    for w in weights[1:3]:
        for c in w:
            c.wait()
    multiply(0, 1, left, both)
    multiply(0, 2, right, both)
    for c in locals_[2:]:
        c.wait()

    tc, ts = twist[0], twist[1]

    def spectrum(load, spec):
        for pair in range(cpd // 2):
            c0, c1 = 2 * pair, 2 * pair + 1
            x = jnp.concatenate([load(c0), load(c1)], axis=1).astype(BF16)
            a = dot(first[...], x)
            for j, c in enumerate((c0, c1)):
                ar = a[:count, j * half:(j + 1) * half]
                ai = a[count:, j * half:(j + 1) * half]
                mid[pl.ds(c * count, count), pl.ds(0, half)] = (ar * tc + ai * ts).astype(BF16)
                mid[pl.ds(c * count, count), pl.ds(half, half)] = (ai * tc - ar * ts).astype(BF16)
        spec[...] = dot(mid[...], second[...])

    def restore(pr, pi, send):
        mid[:, pl.ds(0, half)] = pr.astype(BF16)
        mid[:, pl.ds(half, half)] = pi.astype(BF16)
        spec_g[...] = dot(mid[...], third[...])
        for pair in range(cpd // 2):
            two = []
            for c in (2 * pair, 2 * pair + 1):
                zr = spec_g[pl.ds(c * count, count), pl.ds(0, half)]
                zi = spec_g[pl.ds(c * count, count), pl.ds(half, half)]
                two.append(jnp.concatenate([zr * tc - zi * ts, zi * tc + zr * ts], axis=0).astype(BF16))
            y = dot(last[...], jnp.concatenate(two, axis=1))
            for j in range(2):
                for h in range(2):
                    fwide[pl.ds(h * cpd + 2 * pair + j, n, stride=2 * cpd), :] = (
                        y[h * n:(h + 1) * n, j * half:(j + 1) * half])
        send[...] = fwide[...].astype(BF16).reshape(n, 2 * cpd, half)

    def rows_of(low_ref, low_at, low_stride, high_ref, high_at, high_stride):
        return lambda c: jnp.concatenate(
            [low_ref[pl.ds(low_at + c, n, stride=low_stride), :],
             high_ref[pl.ds(high_at + c, n, stride=high_stride), :]], axis=0)


    def short(h, taps, col):
        cols = pl.ds(col, cl)
        return (
            taps[0:1, :] * proj[pl.ds(HALO + h * half, half), cols]
            + taps[1:2, :] * proj[pl.ds(HALO - 1 + h * half, half), cols]
            + taps[2:3, :] * proj[pl.ds(HALO - 2 + h * half, half), cols]
        )

    def finish(p, cols):
        proj[pl.ds(spans[p].start + HALO, spans[p].size), cols] = acc[spans[p], cols].astype(BF16).astype(F32)

    def gated(h, v):
        at = pl.ds(h * half, half)
        g = short(h, taps_g, cl)
        gate[at, :] = g
        base[at, :] = g * skip[...] * v
        return gout[at, :].astype(F32) * g

    for side in range(2):
        from_far(0, side).wait_recv()
    for c in weights[3]:
        c.wait()
    multiply(0, 3, far, both)
    finish(0, both)
    tail[...] = proj[pl.ds(rows, HALO), :].astype(BF16)
    tail_copy = pltpu.make_async_remote_copy(
        src_ref=tail, dst_ref=tail_in, send_sem=tail_sem.at[0], recv_sem=tail_sem.at[1],
        device_id=(lax.rem(seq + 1, n), ch), device_id_type=MESH,
    )
    tail_copy.start()
    v = short(1, taps_v, 0)
    vsend[1] = v.T.reshape(n, cpd, half).astype(BF16)
    scatter(vsend.at[1], vrecv.at[1], v_sem.at[1])
    vrecv[1, seq] = vsend[1, seq]
    wide[:, pl.ds(cpd, cpd), :] = gated(1, v).T.reshape(n, cpd, half)

    rest(1)
    multiply(1, 1, left, both)
    multiply(1, 2, right, both)
    tail_copy.wait_recv()
    proj[pl.ds(0, HALO), :] = jnp.where(seq > 0, tail_in[...].astype(F32), 0.0)
    value_cols, gate_cols = pl.ds(0, cl), pl.ds(cl, cl)
    for p in range(1, len(pieces)):
        for side in range(2):
            from_far(p, side).wait_recv()
    multiply(1, 3, far, value_cols)
    finish(1, value_cols)
    v = short(0, taps_v, 0)
    vsend[0] = v.T.reshape(n, cpd, half).astype(BF16)
    scatter(vsend.at[0], vrecv.at[0], v_sem.at[0])
    vrecv[0, seq] = vsend[0, seq]
    multiply(1, 3, far, gate_cols)
    finish(1, gate_cols)
    wide[:, pl.ds(0, cpd), :] = gated(0, v).T.reshape(n, cpd, half)
    msend[...] = wide[...].astype(BF16)
    await_all(frecv, f_sem.at[1])
    fwide[...] = frecv[...].astype(F32).reshape(n * 2 * cpd, half)
    spectrum(rows_of(fwide, 0, 2 * cpd, fwide, cpd, 2 * cpd), spec_h)
    scatter(msend, mrecv, m_sem)
    mrecv[seq] = msend[seq]

    for h in (1, 0):
        await_all(vrecv.at[h], v_sem.at[h, 1])
        vwide[h] = vrecv[h].astype(F32).reshape(n * cpd, half)
    spectrum(rows_of(vwide.at[0], 0, cpd, vwide.at[1], 0, cpd), spec_v)
    re, im = pl.ds(0, half), pl.ds(half, half)
    vr, vi = spec_v[:, re], spec_v[:, im]
    hr, hi = spec_h[:, re], spec_h[:, im]
    restore(vr * hr - vi * hi, vr * hi + vi * hr, csend)
    scatter(csend, crecv, c_sem)
    crecv[seq] = csend[seq]

    await_all(mrecv, m_sem.at[1])
    fwide[...] = mrecv[...].astype(F32).reshape(n * 2 * cpd, half)
    spectrum(rows_of(fwide, 0, 2 * cpd, fwide, cpd, 2 * cpd), spec_g)
    gr, gi = spec_g[:, re], spec_g[:, im]
    vr, vi = spec_v[:, re], spec_v[:, im]
    restore(gr * vr + gi * vi, gi * vr - gr * vi, gsend)
    scatter(gsend, grecv, g_sem)
    stays = pltpu.make_async_copy(gsend.at[seq], grecv.at[seq], own_sem.at[0])
    stays.start()

    await_all(crecv, c_sem.at[1])
    wide[...] = crecv[...].astype(F32)
    for h in range(2):
        at = pl.ds(h * half, half)
        y = wide[:, pl.ds(h * cpd, cpd), :].reshape(cl, half).T
        out[at, :] = (gate[at, :] * y + base[at, :]).astype(BF16)
    result = pltpu.make_async_copy(out, out_ref, own_sem.at[1])
    result.start()

    for c in sum(own + onward, [tail_copy]):
        c.wait_send()
    stays.wait()
    result.wait()
    await_all(fsend, f_sem.at[0])
    await_all(msend, m_sem.at[0])
    for h in range(2):
        await_all(vsend.at[h], v_sem.at[h, 0])
    await_all(csend, c_sem.at[0])
    await_all(grecv, g_sem.at[1])
    await_all(gsend, g_sem.at[0])


def closing_kernel(grad_ref, out_in_ref, out_ref, fgrad_ref):
    cpd = grad_ref.shape[1] // 2
    half = grad_ref.shape[2]
    columns = out_ref.shape[1]
    out_ref[...] = out_in_ref[...]
    x = grad_ref[...].astype(F32)
    for h in range(2):
        fgrad_ref[pl.ds(h * half, half), :] = x[:, h * cpd:(h + 1) * cpd, :].reshape(columns, half).T


def shards(n, yn, tokens, w_value, w_gate, short_value, short_gate, skip_bias, long_filter, grad_out):
    rows, dl = tokens.shape
    d, cl = w_value.shape
    half = rows // 2
    cpd = cl // n
    count = 2 * n
    consts = tables(n, half)
    block = (n, 2 * cpd, half)
    small = (n, cpd, half)
    anywhere = pl.BlockSpec(memory_space=pl.ANY)
    dma = pltpu.SemaphoreType.DMA
    scratch = [
        pltpu.VMEM((yn, rows, dl), BF16),
        pltpu.VMEM((d, 2 * cl), BF16),
        pltpu.VMEM((3, cl), F32),
        pltpu.VMEM((3, cl), F32),
        pltpu.VMEM((1, cl), F32),
        pltpu.VMEM((rows, cl), F32),
        pltpu.VMEM((rows, cl), BF16),
        *[pltpu.VMEM(c.shape, c.dtype) for c in consts],
        pltpu.VMEM((rows, 2 * cl), F32),
        pltpu.VMEM((HALO + rows, 2 * cl), F32),
        pltpu.VMEM((HALO, 2 * cl), BF16),
        pltpu.VMEM((HALO, 2 * cl), BF16),
        pltpu.VMEM((rows, cl), F32),
        pltpu.VMEM((rows, cl), F32),
        pltpu.VMEM(block, BF16),
        pltpu.VMEM(block, BF16),
        pltpu.VMEM((2, *small), BF16),
        pltpu.VMEM((2, *small), BF16),
        pltpu.VMEM(block, BF16),
        pltpu.VMEM(block, BF16),
        pltpu.VMEM(block, BF16),
        pltpu.VMEM(block, BF16),
        pltpu.VMEM(block, BF16),
        pltpu.VMEM((rows, cl), BF16),
        pltpu.VMEM(block, F32),
        pltpu.VMEM((n * 2 * cpd, half), F32),
        pltpu.VMEM((2, n * cpd, half), F32),
        pltpu.VMEM((cpd * count, 2 * half), BF16),
        pltpu.VMEM((cpd * count, 2 * half), F32),
        pltpu.VMEM((cpd * count, 2 * half), F32),
        pltpu.VMEM((cpd * count, 2 * half), F32),
        dma((11,)),
        dma((2 * yn,)),
        dma((12,)),
        dma((12,)),
        dma((2,)),
        dma((2,)),
        dma((2,)),
        dma((2, 2)),
        dma((2,)),
        dma((2,)),
        dma((2,)),
        pltpu.SemaphoreType.REGULAR((3,)),
    ]
    grad, out = pl.pallas_call(
        functools.partial(transform_kernel, n, yn),
        out_shape=(
            jax.ShapeDtypeStruct(block, BF16),
            jax.ShapeDtypeStruct((rows, cl), BF16),
        ),
        in_specs=[anywhere] * 13,
        out_specs=[anywhere] * 2,
        scratch_shapes=scratch,
        compiler_params=pltpu.CompilerParams(
            collective_id=0, has_side_effects=True, vmem_limit_bytes=56 * 1024 * 1024
        ),
    )(tokens, w_value, w_gate, short_value, short_gate, skip_bias[None], long_filter, grad_out, *consts)
    steps = 2
    blocks = pl.BlockSpec((n // steps, 2 * cpd, half), lambda i: (i, 0, 0))
    columns = pl.BlockSpec((rows, cl // steps), lambda i: (0, i))
    return pl.pallas_call(
        closing_kernel,
        grid=(steps,),
        out_shape=(
            jax.ShapeDtypeStruct((rows, cl), BF16),
            jax.ShapeDtypeStruct((rows, cl), F32),
        ),
        in_specs=[blocks, columns],
        out_specs=(columns, columns),
    )(grad, out)


def solution(mesh):
    return jax.shard_map(
        functools.partial(shards, mesh.shape["seq"], mesh.shape["ch"]),
        mesh=mesh,
        in_specs=(
            P("seq", "ch"),
            P(None, "ch"),
            P(None, "ch"),
            P(None, "ch"),
            P(None, "ch"),
            P("ch"),
            P("seq", "ch"),
            P("seq", "ch"),
        ),
        out_specs=(P("seq", "ch"), P("seq", "ch")),
        check_vma=False,
    )
```
